32 devices in a mesh: box: 8 (over z, core), agg: 4 (over y, x).
Axes of the slice: x: 2, y: 2, z: 4, core: 2. Of those that a mesh axis runs over, the one named last changes fastest.
Arguments:
- source: float32 [256, 128, 128], P('box', 'agg'), may hold values from -6 to 6
- guess: float32 [256, 128, 128], P('box', 'agg'), may hold values from -6 to 6
- reaction: float32 [256, 128, 128], P('box', 'agg'), may hold values from 0.001 to 0.02
- flags: int32 [8, 4, 4], P('box', 'agg'), may hold values from 0 to 1, as said below
Outputs:
- iterate: float32 [256, 128, 128], P('box', 'agg')
- level_one: float32 [128, 64, 64], P('box', 'agg')
- level_two: float32 [64, 32, 32], P('box', 'agg')
- level_three: float32 [32, 16, 16], P('box', 'agg')
- level_four: float32 [16, 8, 8], P('box', 'agg')
- bottom_residual: float32 [16, 8, 8], P('box', 'agg')
The draws below stay inside these ranges and needn't reach their ends.
Inputs may be any that keep to these rules, and one draw needn't show every extreme that they name: `flags`: flags are 0 or 1; the share of refined boxes differs from device block to device block, and some blocks have none.
All inputs are finite; a program needn't handle non-finite values.
Results may differ from the reference program's by a relative error of at most 0.00018.
Values sent between devices are 32-bit elements; how exact they have to be, the bound alone decides.
A program may use at most 128 MiB of HBM per device.

```python
import math
import jax
import jax.numpy as jnp

CX = 32
CY = 32
CZ = 128
PATCH = 32
LEVELS = 4
NX = 256
NY = 128


def draw_flags(key, part):
    key_device = jax.random.fold_in(key, 11)
    key_boxes = jax.random.fold_in(key, 12)
    refine_level = jax.random.randint(key_device, (NX // CX, NY // CY, 1), 0, 4)
    refine_level = jnp.repeat(jnp.repeat(refine_level, CX // PATCH, axis=0), CY // PATCH, axis=1)
    chance = jax.random.randint(key_boxes, (NX // PATCH, NY // PATCH, CZ // PATCH), 0, 4)
    return (chance < refine_level).astype(jnp.int32)


def block_levels(rng, shape, pieces, smallest, high):
    level, own = 1.0, jax.random.fold_in(rng, 6)
    for dim, blocks in pieces:
        draws = jnp.exp(jax.random.uniform(jax.random.fold_in(own, dim), (blocks,), jnp.float32, smallest / len(pieces), high / len(pieces)))
        level = level * jnp.repeat(draws, shape[dim] // blocks).reshape([-1 if axis == dim else 1 for axis in range(len(shape))])
    return level


def gaussian(own_key, dims, width, most, pieces=(), held_as=jnp.bfloat16):
    entries = jax.random.normal(own_key, dims, jnp.float32) * width
    if len(pieces) > 0:
        entries = block_levels(own_key, dims, pieces, -0.22, 0.18) * entries
    return jnp.clip(entries, min=-most, max=most).astype(held_as)


def setup_inputs(seed: int = 0) -> dict:
    arg_keys = jax.random.split(jax.random.key(seed), 5)
    return {
        "source": gaussian(arg_keys[0], (NX, NY, CZ), 1.0, 6.0, ((0, 8), (1, 4)), jnp.float32),
        "guess": gaussian(arg_keys[1], (NX, NY, CZ), 1.0, 6.0, ((0, 8), (1, 4)), jnp.float32),
        "reaction": jnp.clip(jnp.exp(math.log(0.02) - 2.9957322 * jax.random.uniform(arg_keys[2], (NX, NY, CZ), jnp.float32) ** block_levels(arg_keys[2], (NX, NY, CZ), ((0, 8), (1, 4)), -0.2, 0.2)), 0.001, 0.02),
        "flags": draw_flags(jax.random.fold_in(arg_keys[4], 71), 0),
    }


def neighbours(padded):
    count_x = padded.shape[0] - 2
    count_y = padded.shape[1] - 2
    count_z = padded.shape[2] - 2
    face_sum = jnp.zeros((count_x, count_y, count_z), jnp.float32)
    edge_sum = jnp.zeros((count_x, count_y, count_z), jnp.float32)
    corner_sum = jnp.zeros((count_x, count_y, count_z), jnp.float32)
    for step_x in (-1, 0, 1):
        for step_y in (-1, 0, 1):
            for step_z in (-1, 0, 1):
                moved = abs(step_x) + abs(step_y) + abs(step_z)
                if moved == 0:
                    continue
                window = padded[1 + step_x:1 + step_x + count_x, 1 + step_y:1 + step_y + count_y, 1 + step_z:1 + step_z + count_z]
                if moved == 1:
                    face_sum = face_sum + window
                elif moved == 2:
                    edge_sum = edge_sum + window
                else:
                    corner_sum = corner_sum + window
    return (face_sum + 0.5 * edge_sum + 0.25 * corner_sum) / 14.0


def operate(values, coefficient):
    padded = jnp.pad(values, 1)
    return values - neighbours(padded) + coefficient * values


def restrict(values):
    size_a, size_b, size_c = values.shape
    return values.reshape(size_a // 2, 2, size_b // 2, 2, size_c // 2, 2).sum(axis=(1, 3, 5)) * 0.5


def cell_mask(flags, shape):
    boxes_x, boxes_y, boxes_z = flags.shape
    spread = jnp.broadcast_to(flags.astype(jnp.float32)[:, None, :, None, :, None], (boxes_x, shape[0] // boxes_x, boxes_y, shape[1] // boxes_y, boxes_z, shape[2] // boxes_z))
    return spread.reshape(shape)


def coefficients(level_index):
    upper_edge = 1.1 * (2.0 + 0.02 * 4.0 ** level_index)
    lower_edge = upper_edge / 8.0
    midpoint = (upper_edge + lower_edge) / 2.0
    half_span = (upper_edge - lower_edge) / 2.0
    sigma_value = midpoint / half_span
    rho_first = 1.0 / sigma_value
    rho_second = 1.0 / (2.0 * sigma_value - rho_first)
    return midpoint, rho_second * rho_first, 2.0 * rho_second / half_span


def reference(source, guess, reaction, flags):
    refined = cell_mask(flags, source.shape)
    midpoint, factor_one, factor_two = coefficients(0)
    first_residual = refined * (source - operate(guess, reaction))
    first_step = first_residual / midpoint
    current = guess + first_step
    mid_residual = refined * (source - operate(current, reaction))
    second_step = factor_one * first_step + factor_two * mid_residual
    current = current + second_step
    residual = refined * (source - operate(current, reaction))
    results = [current]
    coarse_reaction = reaction
    for level_index in range(1, LEVELS + 1):
        coarse_source = restrict(residual)
        coarse_reaction = restrict(coarse_reaction)
        midpoint, factor_one, factor_two = coefficients(level_index)
        first_step = coarse_source / midpoint
        mid_residual = coarse_source - operate(first_step, coarse_reaction)
        second_step = factor_one * first_step + factor_two * mid_residual
        correction = first_step + second_step
        residual = coarse_source - operate(correction, coarse_reaction)
        results.append(correction)
    return (results[0], results[1], results[2], results[3], results[4], residual)
```

```python
import functools

import jax
import jax.numpy as jnp
from jax import lax
from jax.experimental import pallas as pl
from jax.experimental.pallas import tpu as pltpu
from jax.sharding import PartitionSpec as P

LEVELS = 4
MESH = pl.DeviceIdType.MESH
NEAR = [(dx, dy) for dx in (-1, 0, 1) for dy in (-1, 0, 1) if (dx, dy) != (0, 0)]
WIDE = [(dx, dy) for dx in range(-2, 3) for dy in range(-2, 3) if (dx, dy) != (0, 0)]


def coefficients(level_index):
    upper_edge = 1.1 * (2.0 + 0.02 * 4.0**level_index)
    lower_edge = upper_edge / 8.0
    midpoint = (upper_edge + lower_edge) / 2.0
    half_span = (upper_edge - lower_edge) / 2.0
    sigma_value = midpoint / half_span
    rho_first = 1.0 / sigma_value
    rho_second = 1.0 / (2.0 * sigma_value - rho_first)
    return (midpoint, rho_second * rho_first, 2.0 * rho_second / half_span)


def row_ids(shape):
    return lax.broadcasted_iota(jnp.int32, shape, len(shape) - 2)


def lane_ids(shape):
    return lax.broadcasted_iota(jnp.int32, shape, len(shape) - 1)


def roll(value, shift, dim):
    size = value.shape[dim]
    shift = shift % size
    return value if shift == 0 else pltpu.roll(value, shift, dim)


def slot_place(slot, width):
    if width == 1:
        return slot, 0
    return 2 * (slot % 4), slot // 4


def slot_mask(slot, width):
    row, half = slot_place(slot, width)
    rows, lanes = row_ids((8, 128)), lane_ids((8, 128))
    mask = (rows >= row) & (rows < row + width)
    if width > 1:
        mask = mask & ((lanes >= 64) if half else (lanes < 64))
    return mask


def unpacked(tile, slot, width, low):
    row, half = slot_place(slot, width)
    rows, lanes = row_ids((8, 128)), lane_ids((8, 128))
    value = roll(tile, (8 - width if low else 0) - row, 0)
    if half:
        value = roll(value, 64, 1)
    mask = (rows >= 8 - width) if low else (rows < width)
    if width > 1:
        mask = mask & (lanes < 64)
    return jnp.where(mask, value, 0.0)


class Halo:
    def __init__(self, place, block, width, packs, sides, corners, send, recv):
        self.place, self.block, self.width = place, block, width
        self.packs, self.sides, self.corners = packs, sides, corners
        self.send, self.recv = send, recv
        self.planes = block.shape[0] - 2 * width
        self.rows = block.shape[1] - 16

    def clear(self):
        w, planes = self.width, self.planes
        edge = jnp.zeros((w,) + self.block.shape[1:], jnp.float32)
        self.block[0:w] = edge
        self.block[planes + w : planes + 2 * w] = edge
        self.sides[...] = jnp.zeros(self.sides.shape, jnp.float32)
        self.corners[...] = jnp.zeros(self.corners.shape, jnp.float32)

    def copy(self, number):
        dx, dy = NEAR[number]
        w, planes, rows, block = self.width, self.planes, self.rows, self.block
        if dy == 0:
            source = block.at[planes : planes + w] if dx > 0 else block.at[w : 2 * w]
            target = block.at[0:w] if dx > 0 else block.at[planes + w : planes + 2 * w]
            source, target = source.at[:, 8 : 8 + rows], target.at[:, 8 : 8 + rows]
        else:
            pack = self.packs.at[0 if dy > 0 else 1]
            if dx == 0:
                source, target = pack, self.sides.at[0 if dy > 0 else 1]
            else:
                source = pack.at[planes // 8 - 1 if dx > 0 else 0]
                target = self.corners.at[(0 if dx > 0 else 2) + (0 if dy > 0 else 1)]
        return pltpu.make_async_remote_copy(
            src_ref=source,
            dst_ref=target,
            send_sem=self.send.at[number],
            recv_sem=self.recv.at[number],
            device_id=self.place.device(dx, dy),
            device_id_type=MESH,
        )

    def start(self):
        w, rows = self.width, self.rows
        for number, (dx, dy) in enumerate(NEAR):
            if dy == 0:
                pl.when(self.place.has(dx, dy))(lambda n=number: self.copy(n).start())
        for tile in range(self.planes // 8):
            high = jnp.zeros((8, 128), jnp.float32)
            low = high
            for slot in range(8):
                row, half = slot_place(slot, w)
                mask = slot_mask(slot, w)
                plane = w + 8 * tile + slot
                last = roll(self.block[plane, rows : rows + 8, :], row + w - 8, 0)
                first = roll(self.block[plane, 8:16, :], row, 0)
                if half:
                    last, first = roll(last, 64, 1), roll(first, 64, 1)
                high = jnp.where(mask, last, high)
                low = jnp.where(mask, first, low)
            self.packs[0, tile] = high
            self.packs[1, tile] = low
        for number, (dx, dy) in enumerate(NEAR):
            if dy != 0:
                pl.when(self.place.has(dx, dy))(lambda n=number: self.copy(n).start())

    def finish(self):
        w, planes, rows = self.width, self.planes, self.rows
        for number, (dx, dy) in enumerate(NEAR):
            pl.when(self.place.has(-dx, -dy))(lambda n=number: self.copy(n).wait_recv())
        for tile in range(planes // 8):
            low, high = self.sides[0, tile], self.sides[1, tile]
            for slot in range(8):
                plane = w + 8 * tile + slot
                self.block[plane, 0:8, :] = unpacked(low, slot, w, True)
                self.block[plane, rows + 8 : rows + 16, :] = unpacked(high, slot, w, False)
        for side in (0, 1):
            low, high = self.corners[2 * side], self.corners[2 * side + 1]
            for index in range(w):
                slot = 8 - w + index if side == 0 else index
                plane = index if side == 0 else planes + w + index
                self.block[plane, 0:8, :] = unpacked(low, slot, w, True)
                self.block[plane, rows + 8 : rows + 16, :] = unpacked(high, slot, w, False)

    def drain(self):
        for number, (dx, dy) in enumerate(NEAR):
            pl.when(self.place.has(dx, dy))(lambda n=number: self.copy(n).wait_send())


class Gather:
    def __init__(self, place, tiles, send, recv):
        self.place, self.tiles, self.send, self.recv = place, tiles, send, recv

    def clear(self):
        self.tiles[...] = jnp.zeros(self.tiles.shape, jnp.float32)

    def copy(self, number):
        dx, dy = WIDE[number]
        return pltpu.make_async_remote_copy(
            src_ref=self.tiles.at[2, 2],
            dst_ref=self.tiles.at[2 - dx, 2 - dy],
            send_sem=self.send.at[number],
            recv_sem=self.recv.at[number],
            device_id=self.place.device(dx, dy),
            device_id_type=MESH,
        )

    def start(self, tile):
        self.tiles[2, 2] = tile
        for number, (dx, dy) in enumerate(WIDE):
            pl.when(self.place.has(dx, dy))(lambda n=number: self.copy(n).start())

    def finish(self, field):
        for number, (dx, dy) in enumerate(WIDE):
            pl.when(self.place.has(-dx, -dy))(lambda n=number: self.copy(n).wait_recv())
        field[...] = jnp.zeros(field.shape, jnp.float32)
        rows, lanes = row_ids((8, 128)), lane_ids((8, 128))
        for bx in range(5):
            for group in range(3):
                pair = [self.tiles[bx, by] for by in range(2 * group, min(2 * group + 2, 5))]
                for index in range(4):
                    total = jnp.zeros((8, 128), jnp.float32)
                    for where, tile in enumerate(pair):
                        value = roll(tile, 4 * where - 4 * (index % 2), 0)
                        if index >= 2:
                            value = roll(value, 64, 1)
                        mask = (rows >= 4 * where) & (rows < 4 * where + 4) & (lanes < 64)
                        total = jnp.where(mask, value, total)
                    field[4 * bx + index, 8 * group : 8 * group + 8, :] = total

    def drain(self):
        for number, (dx, dy) in enumerate(WIDE):
            pl.when(self.place.has(dx, dy))(lambda n=number: self.copy(n).wait_send())


class Place:
    def __init__(self, counts):
        self.counts = counts
        self.box, self.agg = lax.axis_index("box"), lax.axis_index("agg")

    def device(self, dx, dy):
        return (self.box + dx, self.agg + dy)

    def has(self, dx, dy):
        x, y = self.device(dx, dy)
        return (x >= 0) & (x < self.counts[0]) & (y >= 0) & (y < self.counts[1])

    def barrier(self):
        semaphore = pltpu.get_barrier_semaphore()
        for dx, dy in WIDE:

            @pl.when(self.has(dx, dy))
            def _(dx=dx, dy=dy):
                pl.semaphore_signal(
                    semaphore, inc=1, device_id=self.device(dx, dy), device_id_type=MESH
                )

        spans = []
        for at, count in zip((self.box, self.agg), self.counts):
            spans.append(1 + jnp.minimum(at, 2) + jnp.minimum(count - 1 - at, 2))
        pl.semaphore_wait(semaphore, spans[0] * spans[1] - 1)


def weighted(block, plane, wrap):
    middle = block[plane]
    total = (block[plane - 1] + block[plane + 1]) + (middle + middle)
    total = (roll(total, 1, 0) + roll(total, -1, 0)) + (total + total)
    if wrap:
        total = total[8:-8]
        lanes = lane_ids(total.shape)
        left = jnp.where(lanes == 0, 0.0, roll(total, 1, 1))
        right = jnp.where(lanes == 127, 0.0, roll(total, -1, 1))
    else:
        left, right = roll(total, 1, 1), roll(total, -1, 1)
    return (left + right) + (total + total), middle


def paired(flat, extent):
    half = flat.shape[0] // 2
    rows = flat[pl.ds(0, half, stride=2), :] + flat[pl.ds(1, half, stride=2), :]
    source, target = row_ids((128, 128)), lane_ids((128, 128))
    pairs = (source < extent) & ((source == 2 * target) | (source == 2 * target + 1))
    return jnp.dot(
        rows,
        jnp.where(pairs, 0.5, 0.0),
        precision=lax.Precision.HIGHEST,
        preferred_element_type=jnp.float32,
    )


def in_grid(start, stop, shape, extent):
    rows, lanes = row_ids(shape), lane_ids(shape)
    return jnp.where((rows >= start) & (rows < stop) & (lanes < extent), 1.0, 0.0)


def plane_in_grid(index, count):
    return jnp.where((index >= 0) & (index < count), 1.0, 0.0)


def each(start, stop, body, step=2):
    whole = (stop - start) // step

    def several(index, _):
        for offset in range(step):
            body(start + index * step + offset)
        return 0

    lax.fori_loop(0, whole, several, 0)
    for index in range(start + whole * step, stop):
        body(index)


def kernel(
    counts,
    flags, source, guess, reaction,
    iterate, out_one, out_two, out_three, out_four, out_bottom,
    field_a, field_b, field_c, step_one,
    f_one, k_one, e_one, f_two, k_two, e_two,
    f_three, k_three, e_three, f_four, k_four, e_four,
    flat_zero, flat_one, flat_two, flat_three, flat_extra,
    packs_zero, sides_zero, packs_one, sides_one, packs_two, sides_two, corners,
    tiles, near_send, near_recv, wide_send, wide_recv,
):
    place = Place(counts)
    planes, rows, depth = source.shape

    def halo(number, block, width, packs, sides, index):
        return Halo(
            place, block, width, packs.at[index], sides.at[index], corners.at[number],
            near_send.at[number], near_recv.at[number],
        )

    halo_a = halo(0, field_a, 1, packs_zero, sides_zero, 0)
    halo_b = halo(1, field_b, 1, packs_zero, sides_zero, 1)
    halo_c = halo(2, field_c, 1, packs_zero, sides_zero, 2)
    halo_f_one = halo(3, f_one, 2, packs_one, sides_one, 0)
    halo_k_one = halo(4, k_one, 2, packs_one, sides_one, 1)
    halo_f_two = halo(5, f_two, 2, packs_two, sides_two, 0)
    halo_k_two = halo(6, k_two, 2, packs_two, sides_two, 1)
    gather_f = Gather(place, tiles.at[0], wide_send.at[0], wide_recv.at[0])
    gather_k = Gather(place, tiles.at[1], wide_send.at[1], wide_recv.at[1])
    exchanges = [
        halo_a, halo_b, halo_c, halo_f_one, halo_k_one, halo_f_two, halo_k_two, gather_f, gather_k,
    ]
    for exchange in exchanges:
        exchange.clear()

    lanes = lane_ids((rows, depth))
    patch = depth // flags.shape[2]
    refined = jnp.zeros((rows, depth), jnp.float32)
    for box in range(flags.shape[2]):
        chosen = (lanes >= box * patch) & (lanes < (box + 1) * patch)
        refined = refined + jnp.where(chosen, flags[0, 0, box].astype(jnp.float32), 0.0)

    def stage(plane):
        field_a[plane + 1, 8 : 8 + rows, :] = guess[plane]

    each(0, planes, stage, 4)
    place.barrier()
    halo_a.start()

    def spread(flat, target, count, extent):
        values = paired(flat, extent)
        target[2 : 2 + count, 8 : 8 + count, :] = values.reshape(count, count, 128)

    def coarse_reaction(plane):
        flat_zero[pl.ds(pl.multiple_of(plane * rows, rows), rows), :] = (
            reaction[2 * plane] + reaction[2 * plane + 1]
        )

    one, two, three = planes // 2, planes // 4, planes // 8
    each(0, one, coarse_reaction)
    spread(flat_zero, k_one, one, depth)
    halo_k_one.start()
    for plane in range(two):
        flat_one[plane * one : (plane + 1) * one, :] = (
            k_one[2 + 2 * plane, 8 : 8 + one, :] + k_one[3 + 2 * plane, 8 : 8 + one, :]
        )
    spread(flat_one, k_two, two, depth // 2)
    halo_k_two.start()
    for plane in range(three):
        flat_two[plane * two : (plane + 1) * two, :] = (
            k_two[2 + 2 * plane, 8 : 8 + two, :] + k_two[3 + 2 * plane, 8 : 8 + two, :]
        )
    small = paired(flat_two, depth // 4)
    gather_k.start(small[0:8] + roll(small[8:16], 64, 1))

    midpoint, factor_one, factor_two = coefficients(0)

    def fine_residual(block, plane):
        total, middle = weighted(block, plane + 1, True)
        middle = middle[8:-8]
        applied = (8.0 / 7.0 + reaction[plane]) * middle - total * (1.0 / 56.0)
        return refined * (source[plane] - applied), middle

    halo_a.finish()

    def first(plane):
        residual, middle = fine_residual(field_a, plane)
        step = residual * (1.0 / midpoint)
        step_one[plane] = step
        field_b[plane + 1, 8 : 8 + rows, :] = middle + step

    each(0, planes, first)
    halo_b.start()
    halo_b.finish()

    def second(plane):
        residual, middle = fine_residual(field_b, plane)
        value = middle + (factor_one * step_one[plane] + factor_two * residual)
        field_c[plane + 1, 8 : 8 + rows, :] = value
        iterate[plane] = value

    each(0, planes, second)
    halo_c.start()
    halo_c.finish()

    def third(plane):
        total = fine_residual(field_c, 2 * plane)[0] + fine_residual(field_c, 2 * plane + 1)[0]
        flat_zero[pl.ds(pl.multiple_of(plane * rows, rows), rows), :] = total

    each(0, one, third, 1)
    spread(flat_zero, f_one, one, depth)
    halo_f_one.start()

    def correct(level, f, k, e, plane, mask):
        midpoint, factor_one, factor_two = coefficients(level)
        slope = factor_two / midpoint
        keep = (1.0 + factor_one) / midpoint + factor_two - slope * 8.0 / 7.0
        total, middle = weighted(f, plane, False)
        value = (keep - slope * k[plane]) * middle + (slope / 56.0) * total
        e[plane] = value * mask

    def left_over(f, k, e, plane):
        total, middle = weighted(e, plane, False)
        return f[plane] - ((8.0 / 7.0 + k[plane]) * middle - total * (1.0 / 56.0))

    halo_k_one.finish()
    halo_k_two.finish()
    gather_k.finish(k_three)
    for level, f, k, e, exchange, out, flat, size in (
        (1, f_one, k_one, e_one, halo_f_one, out_one, flat_one, one),
        (2, f_two, k_two, e_two, halo_f_two, out_two, flat_two, two),
    ):
        extent = depth >> level
        exchange.finish()
        row_mask = in_grid(
            8 - place.agg * size, 8 + (counts[1] - place.agg) * size, f.shape[1:], extent
        )

        def one_plane(plane, level=level, f=f, k=k, e=e, size=size, row_mask=row_mask):
            at = plane_in_grid(place.box * size + plane - 2, counts[0] * size)
            correct(level, f, k, e, plane, row_mask * at)

        each(1, size + 3, one_plane)
        out[...] = e[2 : 2 + size, 8 : 8 + size, 0:extent]

        def remainder(plane, f=f, k=k, e=e, size=size, flat=flat):
            total = left_over(f, k, e, 2 * plane + 2) + left_over(f, k, e, 2 * plane + 3)
            flat[pl.ds(pl.multiple_of(plane * size, size), size), :] = total[8 : 8 + size]

        each(0, size // 2, remainder, 1)
        if level == 1:
            spread(flat, f_two, size // 2, extent)
            halo_f_two.start()
        else:
            small = paired(flat, extent)
            gather_f.start(small[0:8] + roll(small[8:16], 64, 1))

    gather_f.finish(f_three)
    mask_three = in_grid(
        8 - place.agg * three, 8 + (counts[1] - place.agg) * three, f_three.shape[1:], depth // 8
    )

    def at_three(plane):
        return mask_three * plane_in_grid(place.box * three + plane - 8, counts[0] * three)

    for plane in range(3, 17):
        correct(3, f_three, k_three, e_three, plane, at_three(plane))
    out_three[...] = e_three[8:12, 8:12, 0 : depth // 8]
    flat_three[...] = jnp.zeros(flat_three.shape, jnp.float32)
    flat_extra[...] = jnp.zeros(flat_extra.shape, jnp.float32)
    for plane in range(6):
        total = jnp.zeros(f_three.shape[1:], jnp.float32)
        for child in (4 + 2 * plane, 5 + 2 * plane):
            total = total + left_over(f_three, k_three, e_three, child) * at_three(child)
        flat_three[32 * plane : 32 * plane + 24, :] = total
        flat_extra[32 * plane : 32 * plane + 24, :] = (
            k_three[4 + 2 * plane] + k_three[5 + 2 * plane]
        )
    f_four[...] = paired(flat_three, depth // 8).reshape(6, 16, 128)
    k_four[...] = paired(flat_extra, depth // 8).reshape(6, 16, 128)

    four = three // 2
    mask_four = in_grid(
        4 - place.agg * four, 4 + (counts[1] - place.agg) * four, f_four.shape[1:], depth // 16
    )
    for plane in range(1, 5):
        at = plane_in_grid(place.box * four + plane - 2, counts[0] * four)
        correct(4, f_four, k_four, e_four, plane, mask_four * at)
    out_four[...] = e_four[2:4, 4:6, 0 : depth // 16]
    for plane in (2, 3):
        out_bottom[plane - 2] = left_over(f_four, k_four, e_four, plane)[4:6, 0 : depth // 16]
    for exchange in exchanges:
        exchange.drain()


def per_device(counts, source, guess, reaction, flags):
    planes, rows, depth = source.shape
    assert planes == rows and planes == 32 and depth == 128 and flags.shape[:2] == (1, 1)
    f32 = jnp.float32

    def vmem(*shape):
        return pltpu.VMEM(shape, f32)

    one, two = planes // 2, planes // 4
    scratch = [vmem(planes + 2, rows + 16, depth)] * 3 + [vmem(planes, rows, depth)]
    scratch += [vmem(one + 4, one + 16, 128)] * 3 + [vmem(two + 4, two + 16, 128)] * 3
    scratch += [vmem(20, 24, 128)] * 3 + [vmem(6, 16, 128)] * 3
    scratch += [vmem(one * rows, 128), vmem(two * one, 128), vmem(two // 2 * two, 128)]
    scratch += [vmem(192, 128)] * 2
    scratch += [vmem(3, 2, planes // 8, 8, 128)] * 2
    scratch += [vmem(2, 2, one // 8, 8, 128)] * 2 + [vmem(2, 2, two // 8, 8, 128)] * 2
    scratch += [vmem(7, 4, 8, 128), vmem(2, 5, 5, 8, 128)]
    scratch += [pltpu.SemaphoreType.DMA((7, 8))] * 2 + [pltpu.SemaphoreType.DMA((2, 24))] * 2
    outs = [jax.ShapeDtypeStruct(source.shape, f32)]
    for level in range(1, LEVELS + 1):
        outs.append(
            jax.ShapeDtypeStruct((planes >> level, rows >> level, depth >> level), f32)
        )
    outs.append(outs[-1])
    whole = pl.BlockSpec(memory_space=pltpu.VMEM)
    return tuple(
        pl.pallas_call(
            functools.partial(kernel, counts),
            out_shape=outs,
            in_specs=[pl.BlockSpec(memory_space=pltpu.SMEM)] + [whole] * 3,
            out_specs=[whole] * 6,
            scratch_shapes=scratch,
            compiler_params=pltpu.CompilerParams(
                collective_id=0, has_side_effects=True, vmem_limit_bytes=32 * 1024 * 1024
            ),
        )(flags, source, guess, reaction)
    )


def solution(mesh):
    spec = P("box", "agg", None)
    counts = (mesh.shape["box"], mesh.shape["agg"])
    return jax.shard_map(
        functools.partial(per_device, counts),
        mesh=mesh,
        in_specs=(spec,) * 4,
        out_specs=(spec,) * 6,
        check_vma=False,
    )
```

```python
import functools

import jax
import jax.numpy as jnp
from jax import lax
from jax.experimental import pallas as pl
from jax.experimental.pallas import tpu as pltpu
from jax.sharding import PartitionSpec as P

LEVELS = 4
MESH = pl.DeviceIdType.MESH
NEAR = [(dx, dy) for dx in (-1, 0, 1) for dy in (-1, 0, 1) if (dx, dy) != (0, 0)]
WIDE = [(dx, dy) for dx in range(-2, 3) for dy in range(-2, 3) if (dx, dy) != (0, 0)]


def coefficients(level_index):
    upper_edge = 1.1 * (2.0 + 0.02 * 4.0**level_index)
    lower_edge = upper_edge / 8.0
    midpoint = (upper_edge + lower_edge) / 2.0
    half_span = (upper_edge - lower_edge) / 2.0
    sigma_value = midpoint / half_span
    rho_first = 1.0 / sigma_value
    rho_second = 1.0 / (2.0 * sigma_value - rho_first)
    return (midpoint, rho_second * rho_first, 2.0 * rho_second / half_span)


def row_ids(shape):
    return lax.broadcasted_iota(jnp.int32, shape, len(shape) - 2)


def lane_ids(shape):
    return lax.broadcasted_iota(jnp.int32, shape, len(shape) - 1)


def roll(value, shift, dim):
    size = value.shape[dim]
    shift = shift % size
    return value if shift == 0 else pltpu.roll(value, shift, dim)


def slot_place(slot, width):
    if width == 1:
        return slot, 0
    return 2 * (slot % 4), slot // 4


def slot_mask(slot, width):
    row, half = slot_place(slot, width)
    rows, lanes = row_ids((8, 128)), lane_ids((8, 128))
    mask = (rows >= row) & (rows < row + width)
    if width > 1:
        mask = mask & ((lanes >= 64) if half else (lanes < 64))
    return mask


def unpacked(tile, slot, width, low):
    row, half = slot_place(slot, width)
    rows, lanes = row_ids((8, 128)), lane_ids((8, 128))
    value = roll(tile, (8 - width if low else 0) - row, 0)
    if half:
        value = roll(value, 64, 1)
    mask = (rows >= 8 - width) if low else (rows < width)
    if width > 1:
        mask = mask & (lanes < 64)
    return jnp.where(mask, value, 0.0)


class Halo:
    def __init__(self, place, block, width, packs, sides, corners, send, recv):
        self.place, self.block, self.width = place, block, width
        self.packs, self.sides, self.corners = packs, sides, corners
        self.send, self.recv = send, recv
        self.planes = block.shape[0] - 2 * width
        self.rows = block.shape[1] - 16

    def clear(self):
        w, planes = self.width, self.planes
        edge = jnp.zeros((w,) + self.block.shape[1:], jnp.float32)
        self.block[0:w] = edge
        self.block[planes + w : planes + 2 * w] = edge
        self.sides[...] = jnp.zeros(self.sides.shape, jnp.float32)
        self.corners[...] = jnp.zeros(self.corners.shape, jnp.float32)

    def copy(self, number):
        dx, dy = NEAR[number]
        w, planes, rows, block = self.width, self.planes, self.rows, self.block
        if dy == 0:
            source = block.at[planes : planes + w] if dx > 0 else block.at[w : 2 * w]
            target = block.at[0:w] if dx > 0 else block.at[planes + w : planes + 2 * w]
            source, target = source.at[:, 8 : 8 + rows], target.at[:, 8 : 8 + rows]
        else:
            pack = self.packs.at[0 if dy > 0 else 1]
            if dx == 0:
                source, target = pack, self.sides.at[0 if dy > 0 else 1]
            else:
                source = pack.at[planes // 8 - 1 if dx > 0 else 0]
                target = self.corners.at[(0 if dx > 0 else 2) + (0 if dy > 0 else 1)]
        return pltpu.make_async_remote_copy(
            src_ref=source,
            dst_ref=target,
            send_sem=self.send.at[number],
            recv_sem=self.recv.at[number],
            device_id=self.place.device(dx, dy),
            device_id_type=MESH,
        )

    def start(self):
        w, rows = self.width, self.rows
        for number, (dx, dy) in enumerate(NEAR):
            if dy == 0:
                pl.when(self.place.has(dx, dy))(lambda n=number: self.copy(n).start())
        for tile in range(self.planes // 8):
            high = jnp.zeros((8, 128), jnp.float32)
            low = high
            for slot in range(8):
                row, half = slot_place(slot, w)
                mask = slot_mask(slot, w)
                plane = w + 8 * tile + slot
                last = roll(self.block[plane, rows : rows + 8, :], row + w - 8, 0)
                first = roll(self.block[plane, 8:16, :], row, 0)
                if half:
                    last, first = roll(last, 64, 1), roll(first, 64, 1)
                high = jnp.where(mask, last, high)
                low = jnp.where(mask, first, low)
            self.packs[0, tile] = high
            self.packs[1, tile] = low
        for number, (dx, dy) in enumerate(NEAR):
            if dy != 0:
                pl.when(self.place.has(dx, dy))(lambda n=number: self.copy(n).start())

    def finish(self):
        w, planes, rows = self.width, self.planes, self.rows
        for number, (dx, dy) in enumerate(NEAR):
            pl.when(self.place.has(-dx, -dy))(lambda n=number: self.copy(n).wait_recv())
        for tile in range(planes // 8):
            low, high = self.sides[0, tile], self.sides[1, tile]
            for slot in range(8):
                plane = w + 8 * tile + slot
                self.block[plane, 0:8, :] = unpacked(low, slot, w, True)
                self.block[plane, rows + 8 : rows + 16, :] = unpacked(high, slot, w, False)
        for side in (0, 1):
            low, high = self.corners[2 * side], self.corners[2 * side + 1]
            for index in range(w):
                slot = 8 - w + index if side == 0 else index
                plane = index if side == 0 else planes + w + index
                self.block[plane, 0:8, :] = unpacked(low, slot, w, True)
                self.block[plane, rows + 8 : rows + 16, :] = unpacked(high, slot, w, False)

    def drain(self):
        for number, (dx, dy) in enumerate(NEAR):
            pl.when(self.place.has(dx, dy))(lambda n=number: self.copy(n).wait_send())


class Gather:
    def __init__(self, place, tiles, send, recv):
        self.place, self.tiles, self.send, self.recv = place, tiles, send, recv

    def clear(self):
        self.tiles[...] = jnp.zeros(self.tiles.shape, jnp.float32)

    def copy(self, number):
        dx, dy = WIDE[number]
        return pltpu.make_async_remote_copy(
            src_ref=self.tiles.at[2, 2],
            dst_ref=self.tiles.at[2 - dx, 2 - dy],
            send_sem=self.send.at[number],
            recv_sem=self.recv.at[number],
            device_id=self.place.device(dx, dy),
            device_id_type=MESH,
        )

    def start(self, tile):
        self.tiles[2, 2] = tile
        for number, (dx, dy) in enumerate(WIDE):
            pl.when(self.place.has(dx, dy))(lambda n=number: self.copy(n).start())

    def finish(self, field):
        for number, (dx, dy) in enumerate(WIDE):
            pl.when(self.place.has(-dx, -dy))(lambda n=number: self.copy(n).wait_recv())
        field[...] = jnp.zeros(field.shape, jnp.float32)
        rows, lanes = row_ids((8, 128)), lane_ids((8, 128))
        for bx in range(5):
            for group in range(3):
                pair = [self.tiles[bx, by] for by in range(2 * group, min(2 * group + 2, 5))]
                for index in range(4):
                    total = jnp.zeros((8, 128), jnp.float32)
                    for where, tile in enumerate(pair):
                        value = roll(tile, 4 * where - 4 * (index % 2), 0)
                        if index >= 2:
                            value = roll(value, 64, 1)
                        mask = (rows >= 4 * where) & (rows < 4 * where + 4) & (lanes < 64)
                        total = jnp.where(mask, value, total)
                    field[4 * bx + index, 8 * group : 8 * group + 8, :] = total

    def drain(self):
        for number, (dx, dy) in enumerate(WIDE):
            pl.when(self.place.has(dx, dy))(lambda n=number: self.copy(n).wait_send())


class Place:
    def __init__(self, counts):
        self.counts = counts
        self.box, self.agg = lax.axis_index("box"), lax.axis_index("agg")

    def device(self, dx, dy):
        return (self.box + dx, self.agg + dy)

    def has(self, dx, dy):
        x, y = self.device(dx, dy)
        return (x >= 0) & (x < self.counts[0]) & (y >= 0) & (y < self.counts[1])

    def barrier(self):
        semaphore = pltpu.get_barrier_semaphore()
        for dx, dy in WIDE:

            @pl.when(self.has(dx, dy))
            def _(dx=dx, dy=dy):
                pl.semaphore_signal(
                    semaphore, inc=1, device_id=self.device(dx, dy), device_id_type=MESH
                )

        spans = []
        for at, count in zip((self.box, self.agg), self.counts):
            spans.append(1 + jnp.minimum(at, 2) + jnp.minimum(count - 1 - at, 2))
        pl.semaphore_wait(semaphore, spans[0] * spans[1] - 1)


def weighted(block, start, count, wrap):
    held = [block[start - 1 + index] for index in range(count + 2)]
    pairs = [low + high for low, high in zip(held[:-1], held[1:])]
    results = []
    for index in range(count):
        total = pairs[index] + pairs[index + 1]
        total = (roll(total, 1, 0) + roll(total, -1, 0)) + (total + total)
        middle = held[index + 1]
        if wrap:
            total, middle = total[8:-8], middle[8:-8]
            lanes = lane_ids(total.shape)
            left = jnp.where(lanes == 0, 0.0, roll(total, 1, 1))
            right = jnp.where(lanes == 127, 0.0, roll(total, -1, 1))
        else:
            left, right = roll(total, 1, 1), roll(total, -1, 1)
        results.append(((left + right) + (total + total), middle))
    return results


def paired(flat, extent):
    half = flat.shape[0] // 2
    rows = flat[pl.ds(0, half, stride=2), :] + flat[pl.ds(1, half, stride=2), :]
    high = rows.astype(jnp.bfloat16)
    low = (rows - high.astype(jnp.float32)).astype(jnp.bfloat16)
    source, target = row_ids((256, 128)) % 128, lane_ids((256, 128))
    pairs = (source < extent) & ((source == 2 * target) | (source == 2 * target + 1))
    return jnp.dot(
        jnp.concatenate([high, low], axis=1),
        jnp.where(pairs, 0.5, 0.0).astype(jnp.bfloat16),
        preferred_element_type=jnp.float32,
    )


def in_grid(start, stop, shape, extent):
    rows, lanes = row_ids(shape), lane_ids(shape)
    return jnp.where((rows >= start) & (rows < stop) & (lanes < extent), 1.0, 0.0)


def plane_in_grid(index, count):
    return jnp.where((index >= 0) & (index < count), 1.0, 0.0)


def groups(start, count, size, body):
    assert count % size == 0
    if count == size:
        body(start)
        return

    def step(index, _):
        body(start + index * size)
        return 0

    lax.fori_loop(0, count // size, step, 0)


def kernel(
    counts,
    flags_in, source_in, guess_in, reaction_in,
    iterate, out_one, out_two, out_three, out_four, out_bottom,
    flags, source, reaction,
    field_a, field_b, field_c, step_one,
    f_one, k_one, e_one, f_two, k_two, e_two,
    f_three, k_three, e_three, f_four, k_four, e_four,
    flat_zero, flat_one, flat_two, flat_three, flat_extra,
    packs_zero, sides_zero, packs_one, sides_one, packs_two, sides_two, corners,
    tiles, held_one, held_two, held_three, held_four, held_bottom,
    near_send, near_recv, wide_send, wide_recv, local,
):
    place = Place(counts)
    planes, rows, depth = source.shape

    def halo(number, block, width, packs, sides, index):
        return Halo(
            place, block, width, packs.at[index], sides.at[index], corners.at[number],
            near_send.at[number], near_recv.at[number],
        )

    halo_a = halo(0, field_a, 1, packs_zero, sides_zero, 0)
    halo_b = halo(1, field_b, 1, packs_zero, sides_zero, 1)
    halo_c = halo(2, field_c, 1, packs_zero, sides_zero, 2)
    halo_f_one = halo(3, f_one, 2, packs_one, sides_one, 0)
    halo_k_one = halo(4, k_one, 2, packs_one, sides_one, 1)
    halo_f_two = halo(5, f_two, 2, packs_two, sides_two, 0)
    halo_k_two = halo(6, k_two, 2, packs_two, sides_two, 1)
    gather_f = Gather(place, tiles.at[0], wide_send.at[0], wide_recv.at[0])
    gather_k = Gather(place, tiles.at[1], wide_send.at[1], wide_recv.at[1])
    own_a = field_a.at[1 : 1 + planes, 8 : 8 + rows]
    own_c = field_c.at[1 : 1 + planes, 8 : 8 + rows]
    loads = [
        pltpu.make_async_copy(origin, target, local.at[index])
        for index, (origin, target) in enumerate(
            ((guess_in, own_a), (reaction_in, reaction), (source_in, source), (flags_in, flags))
        )
    ]
    stores = [
        pltpu.make_async_copy(origin, target, local.at[4 + index])
        for index, (origin, target) in enumerate(
            (
                (own_c, iterate), (held_one, out_one), (held_two, out_two),
                (held_three, out_three), (held_four, out_four), (held_bottom, out_bottom),
            )
        )
    ]
    for load in loads:
        load.start()
    for exchange in (
        halo_a, halo_b, halo_c, halo_f_one, halo_k_one, halo_f_two, halo_k_two, gather_f, gather_k,
    ):
        exchange.clear()
    flat_three[...] = jnp.zeros(flat_three.shape, jnp.float32)
    flat_extra[...] = jnp.zeros(flat_extra.shape, jnp.float32)
    place.barrier()
    loads[0].wait()
    halo_a.start()

    def spread(flat, target, count, extent):
        values = paired(flat, extent)
        target[2 : 2 + count, 8 : 8 + count, :] = values.reshape(count, count, 128)

    def put(flat, plane, size, value):
        flat[pl.ds(pl.multiple_of(plane * size, size), size), :] = value

    one, two, three = planes // 2, planes // 4, planes // 8
    loads[1].wait()

    def coarse_reaction(start):
        for plane in range(4):
            at = start + plane
            put(flat_zero, at, rows, reaction[2 * at] + reaction[2 * at + 1])

    groups(0, one, 4, coarse_reaction)
    spread(flat_zero, k_one, one, depth)
    halo_k_one.start()
    loads[2].wait()
    loads[3].wait()

    lanes = lane_ids((1, depth))
    patch = depth // flags.shape[2]
    refined = jnp.zeros((1, depth), jnp.float32)
    for box in range(flags.shape[2]):
        chosen = (lanes >= box * patch) & (lanes < (box + 1) * patch)
        flag = flags[0, :, box : box + 1].astype(jnp.float32)
        refined = refined + jnp.where(chosen, flag, 0.0)

    midpoint, factor_one, factor_two = coefficients(0)

    def fine_residuals(block, start, count):
        results = []
        for index, (total, middle) in enumerate(weighted(block, start + 1, count, True)):
            applied = (8.0 / 7.0 + reaction[start + index]) * middle - total * (1.0 / 56.0)
            results.append((refined * (source[start + index] - applied), middle))
        return results

    halo_a.finish()

    def first(start):
        for index, (residual, middle) in enumerate(fine_residuals(field_a, start, 8)):
            step = residual * (1.0 / midpoint)
            step_one[start + index] = step
            field_b[start + index + 1, 8 : 8 + rows, :] = middle + step

    groups(0, planes, 8, first)
    halo_b.start()

    for plane in range(two):
        put(
            flat_one, plane, one,
            k_one[2 + 2 * plane, 8 : 8 + one, :] + k_one[3 + 2 * plane, 8 : 8 + one, :],
        )
    spread(flat_one, k_two, two, depth // 2)
    halo_k_two.start()
    for plane in range(three):
        put(
            flat_two, plane, two,
            k_two[2 + 2 * plane, 8 : 8 + two, :] + k_two[3 + 2 * plane, 8 : 8 + two, :],
        )
    small = paired(flat_two, depth // 4)
    gather_k.start(small[0:8] + roll(small[8:16], 64, 1))
    halo_b.finish()

    def second(start):
        for index, (residual, middle) in enumerate(fine_residuals(field_b, start, 8)):
            step = factor_one * step_one[start + index] + factor_two * residual
            field_c[start + index + 1, 8 : 8 + rows, :] = middle + step

    groups(0, planes, 8, second)
    halo_c.start()
    stores[0].start()
    halo_k_one.finish()
    halo_k_two.finish()
    halo_a.drain()
    halo_k_one.drain()
    halo_c.finish()

    def third(start):
        values = fine_residuals(field_c, 2 * start, 8)
        for index in range(4):
            put(flat_zero, start + index, rows, values[2 * index][0] + values[2 * index + 1][0])

    groups(0, one, 4, third)
    spread(flat_zero, f_one, one, depth)
    halo_f_one.start()

    def correct(level, f, k, e, start, count, mask):
        midpoint, factor_one, factor_two = coefficients(level)
        slope = factor_two / midpoint
        keep = (1.0 + factor_one) / midpoint + factor_two - slope * 8.0 / 7.0
        for index, (total, middle) in enumerate(weighted(f, start, count, False)):
            plane = start + index
            value = (keep - slope * k[plane]) * middle + (slope / 56.0) * total
            e[plane] = value * mask(plane)

    def left_over(f, k, e, start, count):
        return [
            f[start + index]
            - ((8.0 / 7.0 + k[start + index]) * middle - total * (1.0 / 56.0))
            for index, (total, middle) in enumerate(weighted(e, start, count, False))
        ]

    gather_k.finish(k_three)
    for plane in range(6):
        flat_extra[32 * plane : 32 * plane + 24, :] = (
            k_three[4 + 2 * plane] + k_three[5 + 2 * plane]
        )
    k_four[...] = paired(flat_extra, depth // 8).reshape(6, 16, 128)
    halo_b.drain()
    halo_c.drain()

    for level, f, k, e, exchange, held, flat, size, spans in (
        (1, f_one, k_one, e_one, halo_f_one, held_one, flat_one, one, (6, 4)),
        (2, f_two, k_two, e_two, halo_f_two, held_two, flat_two, two, (10, 4)),
    ):
        extent = depth >> level
        exchange.finish()
        row_mask = in_grid(
            8 - place.agg * size, 8 + (counts[1] - place.agg) * size, f.shape[1:], extent
        )

        def mask(plane, size=size, row_mask=row_mask):
            return row_mask * plane_in_grid(place.box * size + plane - 2, counts[0] * size)

        def ahead(start, level=level, f=f, k=k, e=e, span=spans[0], mask=mask):
            correct(level, f, k, e, start, span, mask)

        groups(1, size + 2, spans[0], ahead)

        def remainder(start, f=f, k=k, e=e, size=size, flat=flat, span=spans[1]):
            values = left_over(f, k, e, 2 * start + 2, 2 * span)
            for index in range(span):
                total = values[2 * index] + values[2 * index + 1]
                put(flat, start + index, size, total[8 : 8 + size])

        groups(0, size // 2, spans[1], remainder)
        if level == 1:
            spread(flat, f_two, size // 2, extent)
            halo_f_two.start()
        else:
            small = paired(flat, extent)
            gather_f.start(small[0:8] + roll(small[8:16], 64, 1))
        held[...] = e[2 : 2 + size, 8 : 8 + size, 0:extent]
        stores[level].start()
        if level == 1:
            halo_k_two.drain()
            gather_k.drain()
        else:
            halo_f_one.drain()
            halo_f_two.drain()

    mask_three = in_grid(
        8 - place.agg * three, 8 + (counts[1] - place.agg) * three, f_three.shape[1:], depth // 8
    )
    ats = {
        plane: plane_in_grid(place.box * three + plane - 8, counts[0] * three)
        for plane in range(3, 17)
    }
    gather_f.finish(f_three)
    correct(3, f_three, k_three, e_three, 3, 14, lambda plane: mask_three * ats[plane])
    held_three[...] = e_three[8:12, 8:12, 0 : depth // 8]
    stores[3].start()
    values = left_over(f_three, k_three, e_three, 4, 12)
    for plane in range(6):
        total = values[2 * plane] * (mask_three * ats[4 + 2 * plane])
        total = total + values[2 * plane + 1] * (mask_three * ats[5 + 2 * plane])
        flat_three[32 * plane : 32 * plane + 24, :] = total
    f_four[...] = paired(flat_three, depth // 8).reshape(6, 16, 128)

    four = three // 2
    mask_four = in_grid(
        4 - place.agg * four, 4 + (counts[1] - place.agg) * four, f_four.shape[1:], depth // 16
    )

    def at_four(plane):
        return mask_four * plane_in_grid(place.box * four + plane - 2, counts[0] * four)

    correct(4, f_four, k_four, e_four, 1, 4, at_four)
    held_four[...] = e_four[2:4, 4:6, 0 : depth // 16]
    stores[4].start()
    for index, value in enumerate(left_over(f_four, k_four, e_four, 2, 2)):
        held_bottom[index] = value[4:6, 0 : depth // 16]
    stores[5].start()
    gather_f.drain()
    for store in stores:
        store.wait()


def hand_on(*refs):
    count = (len(refs) - 1) // 2
    copies = [
        pltpu.make_async_copy(refs[index], refs[count + index], refs[-1].at[index])
        for index in range(count)
    ]
    for copy in copies:
        copy.start()
    for copy in copies:
        copy.wait()


def per_device(counts, source, guess, reaction, flags):
    planes, rows, depth = source.shape
    assert planes == rows and planes == 32 and depth == 128 and flags.shape[:2] == (1, 1)
    f32 = jnp.float32

    def vmem(*shape):
        return pltpu.VMEM(shape, f32)

    one, two = planes // 2, planes // 4
    scratch = [pltpu.VMEM(flags.shape, jnp.int32)] + [vmem(planes, rows, depth)] * 2
    scratch += [vmem(planes + 2, rows + 16, depth)] * 3 + [vmem(planes, rows, depth)]
    scratch += [vmem(one + 4, one + 16, 128)] * 3 + [vmem(two + 4, two + 16, 128)] * 3
    scratch += [vmem(20, 24, 128)] * 3 + [vmem(6, 16, 128)] * 3
    scratch += [vmem(one * rows, 128), vmem(two * one, 128), vmem(two // 2 * two, 128)]
    scratch += [vmem(192, 128)] * 2
    scratch += [vmem(3, 2, planes // 8, 8, 128)] * 2
    scratch += [vmem(2, 2, one // 8, 8, 128)] * 2 + [vmem(2, 2, two // 8, 8, 128)] * 2
    scratch += [vmem(7, 4, 8, 128), vmem(2, 5, 5, 8, 128)]
    outs = [jax.ShapeDtypeStruct(source.shape, f32)]
    for level in range(1, LEVELS + 1):
        outs.append(
            jax.ShapeDtypeStruct((planes >> level, rows >> level, depth >> level), f32)
        )
    outs.append(outs[-1])
    scratch += [vmem(*out.shape) for out in outs[1:]]
    scratch += [pltpu.SemaphoreType.DMA((7, 8))] * 2 + [pltpu.SemaphoreType.DMA((2, 24))] * 2
    scratch += [pltpu.SemaphoreType.DMA((10,))]
    anywhere = pl.BlockSpec(memory_space=pl.ANY)
    results = pl.pallas_call(
        functools.partial(kernel, counts),
        out_shape=outs,
        in_specs=[anywhere] * 4,
        out_specs=[anywhere] * 6,
        scratch_shapes=scratch,
        compiler_params=pltpu.CompilerParams(
            collective_id=0, has_side_effects=True, vmem_limit_bytes=60 * 1024 * 1024
        ),
    )(flags, source, guess, reaction)
    return tuple(
        pl.pallas_call(
            hand_on,
            out_shape=outs,
            in_specs=[anywhere] * 6,
            out_specs=[anywhere] * 6,
            scratch_shapes=[pltpu.SemaphoreType.DMA((6,))],
            compiler_params=pltpu.CompilerParams(vmem_limit_bytes=60 * 1024 * 1024),
        )(*results)
    )


def solution(mesh):
    spec = P("box", "agg", None)
    counts = (mesh.shape["box"], mesh.shape["agg"])
    return jax.shard_map(
        functools.partial(per_device, counts),
        mesh=mesh,
        in_specs=(spec,) * 4,
        out_specs=(spec,) * 6,
        check_vma=False,
    )
```

```python
import functools

import jax
import jax.numpy as jnp
from jax import lax
from jax.experimental import pallas as pl
from jax.experimental.pallas import tpu as pltpu
from jax.sharding import PartitionSpec as P

LEVELS = 4
MESH = pl.DeviceIdType.MESH
NEAR = [(dx, dy) for dx in (-1, 0, 1) for dy in (-1, 0, 1) if (dx, dy) != (0, 0)]
WIDE = [(dx, dy) for dx in range(-2, 3) for dy in range(-2, 3) if (dx, dy) != (0, 0)]


def coefficients(level_index):
    upper_edge = 1.1 * (2.0 + 0.02 * 4.0**level_index)
    lower_edge = upper_edge / 8.0
    midpoint = (upper_edge + lower_edge) / 2.0
    half_span = (upper_edge - lower_edge) / 2.0
    sigma_value = midpoint / half_span
    rho_first = 1.0 / sigma_value
    rho_second = 1.0 / (2.0 * sigma_value - rho_first)
    return (midpoint, rho_second * rho_first, 2.0 * rho_second / half_span)


def row_ids(shape):
    return lax.broadcasted_iota(jnp.int32, shape, len(shape) - 2)


def lane_ids(shape):
    return lax.broadcasted_iota(jnp.int32, shape, len(shape) - 1)


def roll(value, shift, dim):
    size = value.shape[dim]
    shift = shift % size
    return value if shift == 0 else pltpu.roll(value, shift, dim)


def slot_place(slot, width):
    if width == 1:
        return slot, 0
    return 2 * (slot % 4), slot // 4


def slot_mask(slot, width):
    row, half = slot_place(slot, width)
    rows, lanes = row_ids((8, 128)), lane_ids((8, 128))
    mask = (rows >= row) & (rows < row + width)
    if width > 1:
        mask = mask & ((lanes >= 64) if half else (lanes < 64))
    return mask


def unpacked(tile, slot, width, low):
    row, half = slot_place(slot, width)
    rows, lanes = row_ids((8, 128)), lane_ids((8, 128))
    value = roll(tile, (8 - width if low else 0) - row, 0)
    if half:
        value = roll(value, 64, 1)
    mask = (rows >= 8 - width) if low else (rows < width)
    if width > 1:
        mask = mask & (lanes < 64)
    return jnp.where(mask, value, 0.0)


class Halo:
    def __init__(self, place, block, width, packs, sides, corners, send, recv):
        self.place, self.block, self.width = place, block, width
        self.packs, self.sides, self.corners = packs, sides, corners
        self.send, self.recv = send, recv
        self.planes = block.shape[0] - 2 * width
        self.rows = block.shape[1] - 16

    def clear(self):
        w, planes = self.width, self.planes
        edge = jnp.zeros((w,) + self.block.shape[1:], jnp.float32)
        self.block[0:w] = edge
        self.block[planes + w : planes + 2 * w] = edge
        self.sides[...] = jnp.zeros(self.sides.shape, jnp.float32)
        self.corners[...] = jnp.zeros(self.corners.shape, jnp.float32)

    def copy(self, number):
        dx, dy = NEAR[number]
        w, planes, rows, block = self.width, self.planes, self.rows, self.block
        if dy == 0:
            source = block.at[planes : planes + w] if dx > 0 else block.at[w : 2 * w]
            target = block.at[0:w] if dx > 0 else block.at[planes + w : planes + 2 * w]
            source, target = source.at[:, 8 : 8 + rows], target.at[:, 8 : 8 + rows]
        else:
            pack = self.packs.at[0 if dy > 0 else 1]
            if dx == 0:
                source, target = pack, self.sides.at[0 if dy > 0 else 1]
            else:
                source = pack.at[planes // 8 - 1 if dx > 0 else 0]
                target = self.corners.at[(0 if dx > 0 else 2) + (0 if dy > 0 else 1)]
        return pltpu.make_async_remote_copy(
            src_ref=source,
            dst_ref=target,
            send_sem=self.send.at[number],
            recv_sem=self.recv.at[number],
            device_id=self.place.device(dx, dy),
            device_id_type=MESH,
        )

    def start(self):
        w, rows = self.width, self.rows
        for number, (dx, dy) in enumerate(NEAR):
            if dy == 0:
                pl.when(self.place.has(dx, dy))(lambda n=number: self.copy(n).start())
        for tile in range(self.planes // 8):
            high = jnp.zeros((8, 128), jnp.float32)
            low = high
            for slot in range(8):
                row, half = slot_place(slot, w)
                mask = slot_mask(slot, w)
                plane = w + 8 * tile + slot
                last = roll(self.block[plane, rows : rows + 8, :], row + w - 8, 0)
                first = roll(self.block[plane, 8:16, :], row, 0)
                if half:
                    last, first = roll(last, 64, 1), roll(first, 64, 1)
                high = jnp.where(mask, last, high)
                low = jnp.where(mask, first, low)
            self.packs[0, tile] = high
            self.packs[1, tile] = low
        for number, (dx, dy) in enumerate(NEAR):
            if dy != 0:
                pl.when(self.place.has(dx, dy))(lambda n=number: self.copy(n).start())

    def finish(self):
        w, planes, rows = self.width, self.planes, self.rows
        for number, (dx, dy) in enumerate(NEAR):
            pl.when(self.place.has(-dx, -dy))(lambda n=number: self.copy(n).wait_recv())
        for tile in range(planes // 8):
            low, high = self.sides[0, tile], self.sides[1, tile]
            for slot in range(8):
                plane = w + 8 * tile + slot
                self.block[plane, 0:8, :] = unpacked(low, slot, w, True)
                self.block[plane, rows + 8 : rows + 16, :] = unpacked(high, slot, w, False)
        for side in (0, 1):
            low, high = self.corners[2 * side], self.corners[2 * side + 1]
            for index in range(w):
                slot = 8 - w + index if side == 0 else index
                plane = index if side == 0 else planes + w + index
                self.block[plane, 0:8, :] = unpacked(low, slot, w, True)
                self.block[plane, rows + 8 : rows + 16, :] = unpacked(high, slot, w, False)

    def drain(self):
        for number, (dx, dy) in enumerate(NEAR):
            pl.when(self.place.has(dx, dy))(lambda n=number: self.copy(n).wait_send())


class FineHalo(Halo):
    def __init__(self, place, block, packs, sides, corners, outer, send, recv):
        super().__init__(place, block, 1, packs, sides, corners, send, recv)
        self.outer = outer

    def clear(self):
        planes, rows = self.planes, self.rows
        edge = jnp.zeros((1,) + self.block.shape[1:], jnp.float32)
        self.block[0:1] = edge
        self.block[planes + 1 : planes + 2] = edge
        strip = jnp.zeros((planes + 2, 8, 128), jnp.float32)
        self.block[:, 0:8, :] = strip
        self.block[:, 8 + rows : 16 + rows, :] = strip
        for ref in (self.sides, self.corners, self.outer):
            ref[...] = jnp.zeros(ref.shape, jnp.float32)

    def copy(self, number):
        dx, dy = NEAR[number]
        if dy != 0:
            return super().copy(number)
        plane = self.planes if dx > 0 else 1
        return pltpu.make_async_remote_copy(
            src_ref=self.block.at[plane, 8 : 8 + self.rows],
            dst_ref=self.outer.at[0 if dx > 0 else 1, 8 : 8 + self.rows],
            send_sem=self.send.at[number],
            recv_sem=self.recv.at[number],
            device_id=self.place.device(dx, dy),
            device_id_type=MESH,
        )

    def finish(self, refined, scale):
        planes, rows = self.planes, self.rows
        for number, (dx, dy) in enumerate(NEAR):
            pl.when(self.place.has(-dx, -dy))(lambda n=number: self.copy(n).wait_recv())
        factor = refined * scale
        sides, ends = [], []
        for side in (0, 1):
            strip = self.sides[side].reshape(planes, 128)
            at = row_ids(strip.shape)
            before = jnp.where(at == 0, 0.0, roll(strip, 1, 0))
            after = jnp.where(at == planes - 1, 0.0, roll(strip, -1, 0))
            sides.append(factor * along_lanes((before + after) + (strip + strip), True))
        for end in (0, 1):
            slot = 7 if end == 0 else 0
            low, high = self.corners[2 * end], self.corners[2 * end + 1]
            plane = jnp.concatenate(
                [
                    unpacked(low, slot, 1, True),
                    self.outer[end, 8 : 8 + rows, :],
                    unpacked(high, slot, 1, False),
                ],
                axis=0,
            )
            total = (roll(plane, 1, 0) + roll(plane, -1, 0)) + (plane + plane)
            ends.append(factor * along_lanes(total[8 : 8 + rows], True))
        return sides, ends


def edge_tile(strip, plane, last):
    base = plane // 8 * 8
    value = roll(strip[base : base + 8], (7 if last else 0) - plane % 8, 0)
    return jnp.where(row_ids((8, 128)) == (7 if last else 0), value, 0.0)


class Gather:
    def __init__(self, place, tiles, send, recv):
        self.place, self.tiles, self.send, self.recv = place, tiles, send, recv

    def clear(self):
        self.tiles[...] = jnp.zeros(self.tiles.shape, jnp.float32)

    def copy(self, number):
        dx, dy = WIDE[number]
        return pltpu.make_async_remote_copy(
            src_ref=self.tiles.at[2, 2],
            dst_ref=self.tiles.at[2 - dx, 2 - dy],
            send_sem=self.send.at[number],
            recv_sem=self.recv.at[number],
            device_id=self.place.device(dx, dy),
            device_id_type=MESH,
        )

    def start(self, tile):
        self.tiles[2, 2] = tile
        for number, (dx, dy) in enumerate(WIDE):
            pl.when(self.place.has(dx, dy))(lambda n=number: self.copy(n).start())

    def finish(self, field):
        for number, (dx, dy) in enumerate(WIDE):
            pl.when(self.place.has(-dx, -dy))(lambda n=number: self.copy(n).wait_recv())
        field[...] = jnp.zeros(field.shape, jnp.float32)
        rows, lanes = row_ids((8, 128)), lane_ids((8, 128))
        for bx in range(5):
            for group in range(3):
                pair = [self.tiles[bx, by] for by in range(2 * group, min(2 * group + 2, 5))]
                for index in range(4):
                    total = jnp.zeros((8, 128), jnp.float32)
                    for where, tile in enumerate(pair):
                        value = roll(tile, 4 * where - 4 * (index % 2), 0)
                        if index >= 2:
                            value = roll(value, 64, 1)
                        mask = (rows >= 4 * where) & (rows < 4 * where + 4) & (lanes < 64)
                        total = jnp.where(mask, value, total)
                    field[4 * bx + index, 8 * group : 8 * group + 8, :] = total

    def drain(self):
        for number, (dx, dy) in enumerate(WIDE):
            pl.when(self.place.has(dx, dy))(lambda n=number: self.copy(n).wait_send())


class Place:
    def __init__(self, counts):
        self.counts = counts
        self.box, self.agg = lax.axis_index("box"), lax.axis_index("agg")

    def device(self, dx, dy):
        return (self.box + dx, self.agg + dy)

    def has(self, dx, dy):
        x, y = self.device(dx, dy)
        return (x >= 0) & (x < self.counts[0]) & (y >= 0) & (y < self.counts[1])

    def barrier(self):
        semaphore = pltpu.get_barrier_semaphore()
        for dx, dy in WIDE:

            @pl.when(self.has(dx, dy))
            def _(dx=dx, dy=dy):
                pl.semaphore_signal(
                    semaphore, inc=1, device_id=self.device(dx, dy), device_id_type=MESH
                )

        spans = []
        for at, count in zip((self.box, self.agg), self.counts):
            spans.append(1 + jnp.minimum(at, 2) + jnp.minimum(count - 1 - at, 2))
        pl.semaphore_wait(semaphore, spans[0] * spans[1] - 1)


def along_lanes(total, wrap):
    left, right = roll(total, 1, 1), roll(total, -1, 1)
    if wrap:
        lanes = lane_ids(total.shape)
        left = jnp.where(lanes == 0, 0.0, left)
        right = jnp.where(lanes == 127, 0.0, right)
    return (left + right) + (total + total)


def weighted(block, start, count, wrap):
    held = [block[start - 1 + index] for index in range(count + 2)]
    pairs = [low + high for low, high in zip(held[:-1], held[1:])]
    results = []
    for index in range(count):
        total = pairs[index] + pairs[index + 1]
        total = (roll(total, 1, 0) + roll(total, -1, 0)) + (total + total)
        middle = held[index + 1]
        if wrap:
            total, middle = total[8:-8], middle[8:-8]
        results.append((along_lanes(total, wrap), middle))
    return results


def pair_matrix(extent):
    source, target = row_ids((256, 128)) % 128, lane_ids((256, 128))
    pairs = (source < extent) & ((source == 2 * target) | (source == 2 * target + 1))
    return jnp.where(pairs, 0.5, 0.0).astype(jnp.bfloat16)


def paired(flat, matrix):
    half = flat.shape[0] // 2
    rows = flat[pl.ds(0, half, stride=2), :] + flat[pl.ds(1, half, stride=2), :]
    high = rows.astype(jnp.bfloat16)
    low = (rows - high.astype(jnp.float32)).astype(jnp.bfloat16)
    return jnp.dot(
        jnp.concatenate([high, low], axis=1),
        matrix[...],
        preferred_element_type=jnp.float32,
    )


def in_grid(start, stop, shape, extent):
    rows, lanes = row_ids(shape), lane_ids(shape)
    return jnp.where((rows >= start) & (rows < stop) & (lanes < extent), 1.0, 0.0)


def plane_in_grid(index, count):
    return jnp.where((index >= 0) & (index < count), 1.0, 0.0)


def groups(start, count, size, body):
    assert count % size == 0
    if count == size:
        body(start)
        return

    def step(index, _):
        body(start + index * size)
        return 0

    lax.fori_loop(0, count // size, step, 0)


def kernel(
    counts,
    flags_in, source_in, guess_in, reaction_in,
    iterate, out_one, out_two, out_three, out_four, out_bottom,
    flags, source, reaction,
    field_a, field_b, field_c, outer, matrices,
    f_one, k_one, e_one, f_two, k_two, e_two,
    f_three, k_three, e_three, f_four, k_four, e_four,
    flat_zero, flat_one, flat_two, flat_three, flat_extra,
    packs_zero, sides_zero, packs_one, sides_one, packs_two, sides_two, corners,
    tiles, held_one, held_two, held_three, held_four, held_bottom,
    near_send, near_recv, wide_send, wide_recv, local,
):
    place = Place(counts)
    planes, rows, depth = source.shape

    def halo(number, block, width, packs, sides, index):
        return Halo(
            place, block, width, packs.at[index], sides.at[index], corners.at[number],
            near_send.at[number], near_recv.at[number],
        )

    halo_a, halo_b, halo_c = (
        FineHalo(
            place, block, packs_zero.at[index], sides_zero.at[index], corners.at[index],
            outer.at[index], near_send.at[index], near_recv.at[index],
        )
        for index, block in enumerate((field_a, field_b, field_c))
    )
    halo_f_one = halo(3, f_one, 2, packs_one, sides_one, 0)
    halo_k_one = halo(4, k_one, 2, packs_one, sides_one, 1)
    halo_f_two = halo(5, f_two, 2, packs_two, sides_two, 0)
    halo_k_two = halo(6, k_two, 2, packs_two, sides_two, 1)
    gather_f = Gather(place, tiles.at[0], wide_send.at[0], wide_recv.at[0])
    gather_k = Gather(place, tiles.at[1], wide_send.at[1], wide_recv.at[1])
    own_a = field_a.at[1 : 1 + planes, 8 : 8 + rows]
    own_c = field_c.at[1 : 1 + planes, 8 : 8 + rows]
    loads = [
        pltpu.make_async_copy(origin, target, local.at[index])
        for index, (origin, target) in enumerate(
            ((guess_in, own_a), (reaction_in, reaction), (source_in, source), (flags_in, flags))
        )
    ]
    stores = [
        pltpu.make_async_copy(origin, target, local.at[4 + index])
        for index, (origin, target) in enumerate(
            (
                (own_c, iterate), (held_one, out_one), (held_two, out_two),
                (held_three, out_three), (held_four, out_four), (held_bottom, out_bottom),
            )
        )
    ]
    for load in loads:
        load.start()
    for exchange in (
        halo_a, halo_b, halo_c, halo_f_one, halo_k_one, halo_f_two, halo_k_two, gather_f, gather_k,
    ):
        exchange.clear()
    flat_three[...] = jnp.zeros(flat_three.shape, jnp.float32)
    flat_extra[...] = jnp.zeros(flat_extra.shape, jnp.float32)
    for level in range(LEVELS):
        matrices[level] = pair_matrix(depth >> level)
    place.barrier()
    loads[0].wait()
    halo_a.start()

    def spread(flat, target, count, level):
        values = paired(flat, matrices.at[level])
        target[2 : 2 + count, 8 : 8 + count, :] = values.reshape(count, count, 128)

    def put(flat, plane, size, value):
        flat[pl.ds(pl.multiple_of(plane * size, size), size), :] = value

    one, two, three = planes // 2, planes // 4, planes // 8
    loads[1].wait()

    def coarse_reaction(start):
        for plane in range(4):
            at = start + plane
            put(flat_zero, at, rows, reaction[2 * at] + reaction[2 * at + 1])

    groups(0, one, 4, coarse_reaction)
    spread(flat_zero, k_one, one, 0)
    halo_k_one.start()
    loads[2].wait()
    loads[3].wait()

    lanes = lane_ids((1, depth))
    patch = depth // flags.shape[2]
    refined = jnp.zeros((1, depth), jnp.float32)
    for box in range(flags.shape[2]):
        chosen = (lanes >= box * patch) & (lanes < (box + 1) * patch)
        flag = flags[0, :, box : box + 1].astype(jnp.float32)
        refined = refined + jnp.where(chosen, flag, 0.0)

    midpoint, factor_one, factor_two = coefficients(0)

    def fine_residuals(block, start, count):
        results = []
        for index, (total, middle) in enumerate(weighted(block, start + 1, count, True)):
            applied = (8.0 / 7.0 + reaction[start + index]) * middle - total * (1.0 / 56.0)
            results.append((refined * (source[start + index] - applied), middle))
        return results

    def add_edges(block, shares):
        (low, high), ends = shares
        for plane in range(planes):
            block[plane + 1, 8:16, :] += edge_tile(low, plane, False)
            block[plane + 1, rows : 8 + rows, :] += edge_tile(high, plane, True)
        block[1, 8 : 8 + rows, :] += ends[0]
        block[planes, 8 : 8 + rows, :] += ends[1]

    def first(start):
        for index, (residual, middle) in enumerate(fine_residuals(field_a, start, 8)):
            field_b[start + index + 1, 8 : 8 + rows, :] = middle + residual * (1.0 / midpoint)

    groups(0, planes, 8, first)
    add_edges(field_b, halo_a.finish(refined, 1.0 / (56.0 * midpoint)))
    halo_b.start()

    def second(start):
        for index, (residual, middle) in enumerate(fine_residuals(field_b, start, 8)):
            before = field_a[start + index + 1, 8 : 8 + rows, :]
            step = factor_one * (middle - before) + factor_two * residual
            field_c[start + index + 1, 8 : 8 + rows, :] = middle + step

    groups(0, planes, 8, second)
    halo_a.drain()
    add_edges(field_c, halo_b.finish(refined, factor_two / 56.0))
    halo_c.start()
    stores[0].start()

    def third(start):
        values = fine_residuals(field_c, 2 * start, 8)
        for index in range(4):
            put(flat_zero, start + index, rows, values[2 * index][0] + values[2 * index + 1][0])

    groups(0, one, 4, third)
    halo_b.drain()
    halo_k_one.drain()
    (low, high), ends = halo_c.finish(refined, 1.0 / 56.0)
    for plane in range(one):
        at = plane * rows
        for strip, last, begin in ((low, False, at), (high, True, at + rows - 8)):
            both = edge_tile(strip, 2 * plane, last) + edge_tile(strip, 2 * plane + 1, last)
            flat_zero[begin : begin + 8, :] += both
    flat_zero[0:rows, :] += ends[0]
    flat_zero[(one - 1) * rows : one * rows, :] += ends[1]
    spread(flat_zero, f_one, one, 0)
    halo_f_one.start()

    for plane in range(two):
        put(
            flat_one, plane, one,
            k_one[2 + 2 * plane, 8 : 8 + one, :] + k_one[3 + 2 * plane, 8 : 8 + one, :],
        )
    spread(flat_one, k_two, two, 1)
    halo_k_two.start()
    for plane in range(three):
        put(
            flat_two, plane, two,
            k_two[2 + 2 * plane, 8 : 8 + two, :] + k_two[3 + 2 * plane, 8 : 8 + two, :],
        )
    small = paired(flat_two, matrices.at[2])
    gather_k.start(small[0:8] + roll(small[8:16], 64, 1))
    halo_k_one.finish()
    halo_c.drain()

    def correct(level, f, k, e, start, count, mask):
        midpoint, factor_one, factor_two = coefficients(level)
        slope = factor_two / midpoint
        keep = (1.0 + factor_one) / midpoint + factor_two - slope * 8.0 / 7.0
        for index, (total, middle) in enumerate(weighted(f, start, count, False)):
            plane = start + index
            value = (keep - slope * k[plane]) * middle + (slope / 56.0) * total
            e[plane] = value * mask(plane)

    def left_over(f, k, e, start, count):
        return [
            f[start + index]
            - ((8.0 / 7.0 + k[start + index]) * middle - total * (1.0 / 56.0))
            for index, (total, middle) in enumerate(weighted(e, start, count, False))
        ]

    for level, f, k, e, exchange, held, flat, size, spans in (
        (1, f_one, k_one, e_one, halo_f_one, held_one, flat_one, one, (6, 4)),
        (2, f_two, k_two, e_two, halo_f_two, held_two, flat_two, two, (10, 4)),
    ):
        extent = depth >> level
        exchange.finish()
        row_mask = in_grid(
            8 - place.agg * size, 8 + (counts[1] - place.agg) * size, f.shape[1:], extent
        )

        def mask(plane, size=size, row_mask=row_mask):
            return row_mask * plane_in_grid(place.box * size + plane - 2, counts[0] * size)

        def ahead(start, level=level, f=f, k=k, e=e, span=spans[0], mask=mask):
            correct(level, f, k, e, start, span, mask)

        groups(1, size + 2, spans[0], ahead)

        def remainder(start, f=f, k=k, e=e, size=size, flat=flat, span=spans[1]):
            values = left_over(f, k, e, 2 * start + 2, 2 * span)
            for index in range(span):
                total = values[2 * index] + values[2 * index + 1]
                put(flat, start + index, size, total[8 : 8 + size])

        groups(0, size // 2, spans[1], remainder)
        if level == 1:
            spread(flat, f_two, size // 2, level)
            halo_f_two.start()
            halo_k_two.finish()
        else:
            small = paired(flat, matrices.at[level])
            gather_f.start(small[0:8] + roll(small[8:16], 64, 1))
        held[...] = e[2 : 2 + size, 8 : 8 + size, 0:extent]
        stores[level].start()
        if level == 1:
            halo_k_two.drain()
            gather_k.drain()
        else:
            halo_f_one.drain()
            halo_f_two.drain()

    gather_k.finish(k_three)
    for plane in range(6):
        flat_extra[32 * plane : 32 * plane + 24, :] = (
            k_three[4 + 2 * plane] + k_three[5 + 2 * plane]
        )
    k_four[...] = paired(flat_extra, matrices.at[3]).reshape(6, 16, 128)

    mask_three = in_grid(
        8 - place.agg * three, 8 + (counts[1] - place.agg) * three, f_three.shape[1:], depth // 8
    )
    ats = {
        plane: plane_in_grid(place.box * three + plane - 8, counts[0] * three)
        for plane in range(3, 17)
    }
    gather_f.finish(f_three)
    correct(3, f_three, k_three, e_three, 3, 14, lambda plane: mask_three * ats[plane])
    held_three[...] = e_three[8:12, 8:12, 0 : depth // 8]
    stores[3].start()
    values = left_over(f_three, k_three, e_three, 4, 12)
    for plane in range(6):
        total = values[2 * plane] * (mask_three * ats[4 + 2 * plane])
        total = total + values[2 * plane + 1] * (mask_three * ats[5 + 2 * plane])
        flat_three[32 * plane : 32 * plane + 24, :] = total
    f_four[...] = paired(flat_three, matrices.at[3]).reshape(6, 16, 128)

    four = three // 2
    mask_four = in_grid(
        4 - place.agg * four, 4 + (counts[1] - place.agg) * four, f_four.shape[1:], depth // 16
    )

    def at_four(plane):
        return mask_four * plane_in_grid(place.box * four + plane - 2, counts[0] * four)

    correct(4, f_four, k_four, e_four, 1, 4, at_four)
    held_four[...] = e_four[2:4, 4:6, 0 : depth // 16]
    stores[4].start()
    for index, value in enumerate(left_over(f_four, k_four, e_four, 2, 2)):
        held_bottom[index] = value[4:6, 0 : depth // 16]
    stores[5].start()
    gather_f.drain()
    for store in stores:
        store.wait()


def hand_on(*refs):
    sources, targets, held = refs[0:6], refs[6:12], refs[12:18]
    semaphores = refs[18]
    size = sources[0].shape[0] // 4
    parts = [(0, pl.ds(piece * size, size)) for piece in range(4)]
    parts += [(index, pl.ds(0, sources[index].shape[0])) for index in range(1, 6)]
    inward, outward = [], []
    for number, (index, part) in enumerate(parts):
        inner = held[index].at[part]
        inward.append(
            pltpu.make_async_copy(sources[index].at[part], inner, semaphores.at[0, number])
        )
        outward.append(
            pltpu.make_async_copy(inner, targets[index].at[part], semaphores.at[1, number])
        )
    for copy in inward:
        copy.start()
    for before, after in zip(inward, outward):
        before.wait()
        after.start()
    for copy in outward:
        copy.wait()


def per_device(counts, source, guess, reaction, flags):
    planes, rows, depth = source.shape
    assert planes == rows and planes == 32 and depth == 128 and flags.shape[:2] == (1, 1)
    f32 = jnp.float32

    def vmem(*shape):
        return pltpu.VMEM(shape, f32)

    one, two = planes // 2, planes // 4
    scratch = [pltpu.VMEM(flags.shape, jnp.int32)] + [vmem(planes, rows, depth)] * 2
    scratch += [vmem(planes + 2, rows + 16, depth)] * 3 + [vmem(3, 2, rows + 16, depth)]
    scratch += [pltpu.VMEM((LEVELS, 256, 128), jnp.bfloat16)]
    scratch += [vmem(one + 4, one + 16, 128)] * 3 + [vmem(two + 4, two + 16, 128)] * 3
    scratch += [vmem(20, 24, 128)] * 3 + [vmem(6, 16, 128)] * 3
    scratch += [vmem(one * rows, 128), vmem(two * one, 128), vmem(two // 2 * two, 128)]
    scratch += [vmem(192, 128)] * 2
    scratch += [vmem(3, 2, planes // 8, 8, 128)] * 2
    scratch += [vmem(2, 2, one // 8, 8, 128)] * 2 + [vmem(2, 2, two // 8, 8, 128)] * 2
    scratch += [vmem(7, 4, 8, 128), vmem(2, 5, 5, 8, 128)]
    outs = [jax.ShapeDtypeStruct(source.shape, f32)]
    for level in range(1, LEVELS + 1):
        outs.append(
            jax.ShapeDtypeStruct((planes >> level, rows >> level, depth >> level), f32)
        )
    outs.append(outs[-1])
    scratch += [vmem(*out.shape) for out in outs[1:]]
    scratch += [pltpu.SemaphoreType.DMA((7, 8))] * 2 + [pltpu.SemaphoreType.DMA((2, 24))] * 2
    scratch += [pltpu.SemaphoreType.DMA((10,))]
    anywhere = pl.BlockSpec(memory_space=pl.ANY)
    results = pl.pallas_call(
        functools.partial(kernel, counts),
        out_shape=outs,
        in_specs=[anywhere] * 4,
        out_specs=[anywhere] * 6,
        scratch_shapes=scratch,
        compiler_params=pltpu.CompilerParams(
            collective_id=0, has_side_effects=True, vmem_limit_bytes=60 * 1024 * 1024
        ),
    )(flags, source, guess, reaction)
    return tuple(
        pl.pallas_call(
            hand_on,
            out_shape=outs,
            in_specs=[anywhere] * 6,
            out_specs=[anywhere] * 6,
            scratch_shapes=[vmem(*out.shape) for out in outs] + [pltpu.SemaphoreType.DMA((2, 9))],
            compiler_params=pltpu.CompilerParams(vmem_limit_bytes=60 * 1024 * 1024),
        )(*results)
    )


def solution(mesh):
    spec = P("box", "agg", None)
    counts = (mesh.shape["box"], mesh.shape["agg"])
    return jax.shard_map(
        functools.partial(per_device, counts),
        mesh=mesh,
        in_specs=(spec,) * 4,
        out_specs=(spec,) * 6,
        check_vma=False,
    )
```

```python
import functools

import jax
import jax.numpy as jnp
from jax import lax
from jax.experimental import pallas as pl
from jax.experimental.pallas import tpu as pltpu
from jax.sharding import PartitionSpec as P

LEVELS = 4
MESH = pl.DeviceIdType.MESH
NEAR = [(dx, dy) for dx in (-1, 0, 1) for dy in (-1, 0, 1) if (dx, dy) != (0, 0)]


def coefficients(level_index):
    upper_edge = 1.1 * (2.0 + 0.02 * 4.0**level_index)
    lower_edge = upper_edge / 8.0
    midpoint = (upper_edge + lower_edge) / 2.0
    half_span = (upper_edge - lower_edge) / 2.0
    sigma_value = midpoint / half_span
    rho_first = 1.0 / sigma_value
    rho_second = 1.0 / (2.0 * sigma_value - rho_first)
    return (midpoint, rho_second * rho_first, 2.0 * rho_second / half_span)


def row_ids(shape):
    return lax.broadcasted_iota(jnp.int32, shape, len(shape) - 2)


def lane_ids(shape):
    return lax.broadcasted_iota(jnp.int32, shape, len(shape) - 1)


def roll(value, shift, dim):
    size = value.shape[dim]
    shift = shift % size
    return value if shift == 0 else pltpu.roll(value, shift, dim)


def slot_place(slot, width):
    if width == 1:
        return slot, 0
    return 2 * (slot % 4), slot // 4


def slot_mask(slot, width):
    row, half = slot_place(slot, width)
    rows, lanes = row_ids((8, 128)), lane_ids((8, 128))
    mask = (rows >= row) & (rows < row + width)
    if width > 1:
        mask = mask & ((lanes >= 64) if half else (lanes < 64))
    return mask


def unpacked(tile, slot, width, low):
    row, half = slot_place(slot, width)
    rows, lanes = row_ids((8, 128)), lane_ids((8, 128))
    value = roll(tile, (8 - width if low else 0) - row, 0)
    if half:
        value = roll(value, 64, 1)
    mask = (rows >= 8 - width) if low else (rows < width)
    if width > 1:
        mask = mask & (lanes < 64)
    return jnp.where(mask, value, 0.0)


def pack_edges(block, width, high, low):
    planes, rows = block.shape[0] - 2 * width, block.shape[1] - 16
    for tile in range(planes // 8):
        upper = jnp.zeros((8, 128), jnp.float32)
        lower = upper
        for slot in range(8):
            row, half = slot_place(slot, width)
            mask = slot_mask(slot, width)
            plane = width + 8 * tile + slot
            last = roll(block[plane, rows : rows + 8, :], row + width - 8, 0)
            first = roll(block[plane, 8:16, :], row, 0)
            if half:
                last, first = roll(last, 64, 1), roll(first, 64, 1)
            upper = jnp.where(mask, last, upper)
            lower = jnp.where(mask, first, lower)
        high[tile] = upper
        low[tile] = lower


def unpack_edges(block, width, tile, low, high):
    rows = block.shape[1] - 16
    for slot in range(8):
        plane = width + 8 * tile + slot
        block[plane, 0:8, :] = unpacked(low, slot, width, True)
        block[plane, rows + 8 : rows + 16, :] = unpacked(high, slot, width, False)


def unpack_corners(block, width, side, low, high):
    planes, rows = block.shape[0] - 2 * width, block.shape[1] - 16
    for index in range(width):
        slot = 8 - width + index if side == 0 else index
        plane = index if side == 0 else planes + width + index
        block[plane, 0:8, :] = unpacked(low, slot, width, True)
        block[plane, rows + 8 : rows + 16, :] = unpacked(high, slot, width, False)


class Halo:
    def __init__(self, place, block, width, packs, sides, corners, send, recv):
        self.place, self.block, self.width = place, block, width
        self.packs, self.sides, self.corners = packs, sides, corners
        self.send, self.recv = send, recv
        self.planes = block.shape[0] - 2 * width
        self.rows = block.shape[1] - 16

    def clear(self):
        w, planes = self.width, self.planes
        edge = jnp.zeros((w,) + self.block.shape[1:], jnp.float32)
        self.block[0:w] = edge
        self.block[planes + w : planes + 2 * w] = edge
        self.sides[...] = jnp.zeros(self.sides.shape, jnp.float32)
        self.corners[...] = jnp.zeros(self.corners.shape, jnp.float32)

    def copy(self, number):
        dx, dy = NEAR[number]
        w, planes, rows, block = self.width, self.planes, self.rows, self.block
        if dy == 0:
            source = block.at[planes : planes + w] if dx > 0 else block.at[w : 2 * w]
            target = block.at[0:w] if dx > 0 else block.at[planes + w : planes + 2 * w]
            source, target = source.at[:, 8 : 8 + rows], target.at[:, 8 : 8 + rows]
        else:
            pack = self.packs.at[0 if dy > 0 else 1]
            if dx == 0:
                source, target = pack, self.sides.at[0 if dy > 0 else 1]
            else:
                source = pack.at[planes // 8 - 1 if dx > 0 else 0]
                target = self.corners.at[(0 if dx > 0 else 2) + (0 if dy > 0 else 1)]
        return pltpu.make_async_remote_copy(
            src_ref=source,
            dst_ref=target,
            send_sem=self.send.at[number],
            recv_sem=self.recv.at[number],
            device_id=self.place.device(dx, dy),
            device_id_type=MESH,
        )

    def start(self):
        for number, (dx, dy) in enumerate(NEAR):
            if dy == 0:
                pl.when(self.place.has(dx, dy))(lambda n=number: self.copy(n).start())
        pack_edges(self.block, self.width, self.packs.at[0], self.packs.at[1])
        for number, (dx, dy) in enumerate(NEAR):
            if dy != 0:
                pl.when(self.place.has(dx, dy))(lambda n=number: self.copy(n).start())

    def finish(self):
        self.arrive()
        for tile in range(self.planes // 8):
            unpack_edges(self.block, self.width, tile, self.sides[0, tile], self.sides[1, tile])
        for side in (0, 1):
            low, high = self.corners[2 * side], self.corners[2 * side + 1]
            unpack_corners(self.block, self.width, side, low, high)

    def arrive(self):
        for number, (dx, dy) in enumerate(NEAR):
            pl.when(self.place.has(-dx, -dy))(lambda n=number: self.copy(n).wait_recv())

    def drain(self):
        for number, (dx, dy) in enumerate(NEAR):
            pl.when(self.place.has(dx, dy))(lambda n=number: self.copy(n).wait_send())


class FineHalo(Halo):
    def __init__(self, place, block, packs, sides, corners, outer, send, recv):
        super().__init__(place, block, 1, packs, sides, corners, send, recv)
        self.outer = outer

    def clear(self):
        planes, rows = self.planes, self.rows
        edge = jnp.zeros((1,) + self.block.shape[1:], jnp.float32)
        self.block[0:1] = edge
        self.block[planes + 1 : planes + 2] = edge
        strip = jnp.zeros((planes + 2, 8, 128), jnp.float32)
        self.block[:, 0:8, :] = strip
        self.block[:, 8 + rows : 16 + rows, :] = strip
        for ref in (self.sides, self.corners, self.outer):
            ref[...] = jnp.zeros(ref.shape, jnp.float32)

    def copy(self, number):
        dx, dy = NEAR[number]
        if dy != 0:
            return super().copy(number)
        plane = self.planes if dx > 0 else 1
        return pltpu.make_async_remote_copy(
            src_ref=self.block.at[plane, 8 : 8 + self.rows],
            dst_ref=self.outer.at[0 if dx > 0 else 1, 8 : 8 + self.rows],
            send_sem=self.send.at[number],
            recv_sem=self.recv.at[number],
            device_id=self.place.device(dx, dy),
            device_id_type=MESH,
        )

    def finish(self, refined, scale):
        planes, rows = self.planes, self.rows
        for number, (dx, dy) in enumerate(NEAR):
            pl.when(self.place.has(-dx, -dy))(lambda n=number: self.copy(n).wait_recv())
        factor = refined * scale
        sides, ends = [], []
        for side in (0, 1):
            strip = self.sides[side].reshape(planes, 128)
            at = row_ids(strip.shape)
            before = jnp.where(at == 0, 0.0, roll(strip, 1, 0))
            after = jnp.where(at == planes - 1, 0.0, roll(strip, -1, 0))
            sides.append(factor * along_lanes((before + after) + (strip + strip), True))
        for end in (0, 1):
            slot = 7 if end == 0 else 0
            low, high = self.corners[2 * end], self.corners[2 * end + 1]
            plane = jnp.concatenate(
                [
                    unpacked(low, slot, 1, True),
                    self.outer[end, 8 : 8 + rows, :],
                    unpacked(high, slot, 1, False),
                ],
                axis=0,
            )
            total = (roll(plane, 1, 0) + roll(plane, -1, 0)) + (plane + plane)
            ends.append(factor * along_lanes(total[8 : 8 + rows], True))
        return sides, ends


def edge_tile(strip, plane, last):
    base = plane // 8 * 8
    value = roll(strip[base : base + 8], (7 if last else 0) - plane % 8, 0)
    return jnp.where(row_ids((8, 128)) == (7 if last else 0), value, 0.0)


class Coefficients(Halo):
    def __init__(self, place, fields, packs, ends, sides, corners, outer, send, recv):
        self.place, self.fields = place, fields
        self.packs, self.ends = packs, ends
        self.sides, self.corners, self.outer = sides, corners, outer
        self.send, self.recv = send, recv

    def clear(self):
        for ref in (self.sides, self.corners, self.outer):
            ref[...] = jnp.zeros(ref.shape, jnp.float32)

    def copy(self, number):
        dx, dy = NEAR[number]
        across, along = (0 if dx > 0 else 1), (0 if dy > 0 else 1)
        if dy == 0:
            source, target = self.ends.at[across], self.outer.at[across]
        else:
            source = self.packs.at[along]
            target = self.sides.at[along] if dx == 0 else self.corners.at[2 * across + along]
        return pltpu.make_async_remote_copy(
            src_ref=source,
            dst_ref=target,
            send_sem=self.send.at[number],
            recv_sem=self.recv.at[number],
            device_id=self.place.device(dx, dy),
            device_id_type=MESH,
        )

    def start(self, tile):
        self.tile = tile
        at = 0
        for block in self.fields:
            size = (block.shape[0] - 4) // 8
            part = pl.ds(at, size)
            pack_edges(block, 2, self.packs.at[0, part], self.packs.at[1, part])
            at += size
        at = 0
        for block in self.fields:
            planes, rows = block.shape[0] - 4, block.shape[1] - 16
            size = rows // 8
            for index in range(2):
                for across, plane in ((0, planes + index), (1, 2 + index)):
                    value = block[plane, 8 : 8 + rows, :].reshape(size, 8, 128)
                    self.ends[across, at : at + size] = value
                at += size
        for ref in (self.packs, self.ends):
            for index in range(2):
                ref[index, ref.shape[1] - 1] = tile
        for number, (dx, dy) in enumerate(NEAR):
            pl.when(self.place.has(dx, dy))(lambda n=number: self.copy(n).start())

    def finish(self, third):
        self.arrive()
        at, end = 0, 0
        for block in self.fields:
            planes, rows = block.shape[0] - 4, block.shape[1] - 16
            count, size = planes // 8, rows // 8
            for tile in range(count):
                low, high = self.sides[0, at + tile], self.sides[1, at + tile]
                unpack_edges(block, 2, tile, low, high)
            for side in (0, 1):
                tile = at + (count - 1 if side == 0 else 0)
                low, high = self.corners[2 * side, tile], self.corners[2 * side + 1, tile]
                unpack_corners(block, 2, side, low, high)
                for index in range(2):
                    plane = index if side == 0 else planes + 2 + index
                    first = end + index * size
                    value = self.outer[side, first : first + size].reshape(rows, 128)
                    block[plane, 8 : 8 + rows, :] = value
            at += count
            end += 2 * size
        around = [
            [self.corners[0, at], self.outer[0, end], self.corners[1, at]],
            [self.sides[0, at], self.tile, self.sides[1, at]],
            [self.corners[2, at], self.outer[1, end], self.corners[3, at]],
        ]
        lay_out(around, third)


def lay_out(around, field):
    rows, lanes = row_ids((8, 128)), lane_ids((8, 128))
    for bx in range(3):
        for index in range(4):
            values = []
            for by in range(3):
                value = roll(around[bx][by], 4 * (by % 2) - 4 * (index % 2), 0)
                values.append(roll(value, 64, 1) if index >= 2 else value)
            head = jnp.where(rows < 4, values[0], values[1])
            tail = jnp.where(rows < 4, values[2], 0.0)
            field[4 * bx + index, 0:8, :] = jnp.where(lanes < 64, head, 0.0)
            field[4 * bx + index, 8:16, :] = jnp.where(lanes < 64, tail, 0.0)


class Gather(Halo):
    def __init__(self, place, tiles, send, recv):
        self.place, self.tiles, self.send, self.recv = place, tiles, send, recv

    def clear(self):
        self.tiles[...] = jnp.zeros(self.tiles.shape, jnp.float32)

    def copy(self, number):
        dx, dy = NEAR[number]
        return pltpu.make_async_remote_copy(
            src_ref=self.tiles.at[1, 1],
            dst_ref=self.tiles.at[1 - dx, 1 - dy],
            send_sem=self.send.at[number],
            recv_sem=self.recv.at[number],
            device_id=self.place.device(dx, dy),
            device_id_type=MESH,
        )

    def start(self):
        for number, (dx, dy) in enumerate(NEAR):
            pl.when(self.place.has(dx, dy))(lambda n=number: self.copy(n).start())


class Place:
    def __init__(self, counts):
        self.counts = counts
        self.box, self.agg = lax.axis_index("box"), lax.axis_index("agg")

    def device(self, dx, dy):
        return (self.box + dx, self.agg + dy)

    def has(self, dx, dy):
        x, y = self.device(dx, dy)
        return (x >= 0) & (x < self.counts[0]) & (y >= 0) & (y < self.counts[1])

    def greet(self):
        semaphore = pltpu.get_barrier_semaphore()
        for dx, dy in NEAR:

            @pl.when(self.has(dx, dy))
            def _(dx=dx, dy=dy):
                pl.semaphore_signal(
                    semaphore, inc=1, device_id=self.device(dx, dy), device_id_type=MESH
                )

    def await_greetings(self):
        spans = []
        for at, count in zip((self.box, self.agg), self.counts):
            spans.append(1 + jnp.minimum(at, 1) + jnp.minimum(count - 1 - at, 1))
        pl.semaphore_wait(pltpu.get_barrier_semaphore(), spans[0] * spans[1] - 1)


def along_lanes(total, wrap):
    left, right = roll(total, 1, 1), roll(total, -1, 1)
    if wrap:
        lanes = lane_ids(total.shape)
        left = jnp.where(lanes == 0, 0.0, left)
        right = jnp.where(lanes == 127, 0.0, right)
    return (left + right) + (total + total)


def weighted(block, start, count, wrap):
    held = [block[start - 1 + index] for index in range(count + 2)]
    pairs = [low + high for low, high in zip(held[:-1], held[1:])]
    results = []
    for index in range(count):
        total = pairs[index] + pairs[index + 1]
        total = (roll(total, 1, 0) + roll(total, -1, 0)) + (total + total)
        middle = held[index + 1]
        if wrap:
            total, middle = total[8:-8], middle[8:-8]
        results.append((along_lanes(total, wrap), middle))
    return results


def pair_matrix(extent):
    source, target = row_ids((256, 128)) % 128, lane_ids((256, 128))
    pairs = (source < extent) & ((source == 2 * target) | (source == 2 * target + 1))
    return jnp.where(pairs, 0.5, 0.0).astype(jnp.bfloat16)


def paired(flat, matrix):
    half = flat.shape[0] // 2
    rows = flat[pl.ds(0, half, stride=2), :] + flat[pl.ds(1, half, stride=2), :]
    high = rows.astype(jnp.bfloat16)
    low = (rows - high.astype(jnp.float32)).astype(jnp.bfloat16)
    return jnp.dot(
        jnp.concatenate([high, low], axis=1),
        matrix[...],
        preferred_element_type=jnp.float32,
    )


def in_grid(start, stop, shape, extent):
    rows, lanes = row_ids(shape), lane_ids(shape)
    return jnp.where((rows >= start) & (rows < stop) & (lanes < extent), 1.0, 0.0)


def plane_in_grid(index, count):
    return jnp.where((index >= 0) & (index < count), 1.0, 0.0)


def groups(start, count, size, body):
    assert count % size == 0
    if count == size:
        body(start)
        return

    def step(index, _):
        body(start + index * size)
        return 0

    lax.fori_loop(0, count // size, step, 0)


def kernel(
    counts,
    flags_in, source_in, guess_in, reaction_in,
    iterate, out_one, out_two, out_three, out_four, out_bottom,
    flags, source, reaction,
    field_a, field_b, field_c, outer, matrices,
    f_one, k_one, e_one, f_two, k_two, e_two,
    f_three, k_three, e_three, f_four, k_four, e_four,
    flat_zero, flat_one, flat_two, flat_three, flat_extra,
    packs_zero, sides_zero, packs_one, sides_one, packs_two, sides_two, corners,
    k_packs, k_ends, k_sides, k_corners, k_outer, tiles_three, tiles_four, held_one, held_two, held_three, held_four, held_bottom,
    near_send, near_recv, local,
):
    place = Place(counts)
    planes, rows, depth = source.shape

    def halo(number, block, width, packs, sides, index):
        return Halo(
            place, block, width, packs.at[index], sides.at[index], corners.at[number],
            near_send.at[number], near_recv.at[number],
        )

    halo_a, halo_b, halo_c = (
        FineHalo(
            place, block, packs_zero.at[index], sides_zero.at[index], corners.at[index],
            outer.at[index], near_send.at[index], near_recv.at[index],
        )
        for index, block in enumerate((field_a, field_b, field_c))
    )
    halo_f_one = halo(3, f_one, 2, packs_one, sides_one, 0)
    halo_f_two = halo(4, f_two, 2, packs_two, sides_two, 0)
    halo_k = Coefficients(
        place, (k_one, k_two), k_packs, k_ends, k_sides, k_corners, k_outer,
        near_send.at[5], near_recv.at[5],
    )
    gather_three = Gather(place, tiles_three, near_send.at[6], near_recv.at[6])
    gather_four = Gather(place, tiles_four, near_send.at[7], near_recv.at[7])
    own_a = field_a.at[1 : 1 + planes, 8 : 8 + rows]
    own_c = field_c.at[1 : 1 + planes, 8 : 8 + rows]
    quarter = planes // 4
    parts = [pl.ds(index * quarter, quarter) for index in range(4)]
    pairs = [(guess_in.at[part], own_a.at[part]) for part in parts]
    pairs += [(flags_in, flags)]
    pairs += [(reaction_in.at[part], reaction.at[part]) for part in parts]
    pairs += [(source_in.at[part], source.at[part]) for part in parts]
    loads = [
        pltpu.make_async_copy(origin, target, local.at[6 + index])
        for index, (origin, target) in enumerate(pairs)
    ]
    stores = [
        pltpu.make_async_copy(origin, target, local.at[index])
        for index, (origin, target) in enumerate(
            (
                (own_c, iterate), (held_one, out_one), (held_two, out_two),
                (held_three, out_three), (held_four, out_four), (held_bottom, out_bottom),
            )
        )
    ]
    for load in loads[:4]:
        load.start()
    for exchange in (
        halo_a, halo_b, halo_c, halo_f_one, halo_f_two, halo_k, gather_three, gather_four,
    ):
        exchange.clear()
    place.greet()
    for load in loads[4:]:
        load.start()
    for level in range(LEVELS):
        matrices[level] = pair_matrix(depth >> level)
    for load in loads[:4]:
        load.wait()
    place.await_greetings()
    halo_a.start()

    def spread(flat, target, count, level):
        values = paired(flat, matrices.at[level])
        target[2 : 2 + count, 8 : 8 + count, :] = values.reshape(count, count, 128)

    def put(flat, plane, size, value):
        flat[pl.ds(pl.multiple_of(plane * size, size), size), :] = value

    one, two, three = planes // 2, planes // 4, planes // 8
    for load in loads[4:9]:
        load.wait()

    def coarse_reaction(start):
        for plane in range(4):
            at = start + plane
            put(flat_zero, at, rows, reaction[2 * at] + reaction[2 * at + 1])

    groups(0, one, 4, coarse_reaction)
    spread(flat_zero, k_one, one, 0)
    for load in loads[9:]:
        load.wait()

    lanes = lane_ids((1, depth))
    patch = depth // flags.shape[2]
    refined = jnp.zeros((1, depth), jnp.float32)
    for box in range(flags.shape[2]):
        chosen = (lanes >= box * patch) & (lanes < (box + 1) * patch)
        flag = flags[0, :, box : box + 1].astype(jnp.float32)
        refined = refined + jnp.where(chosen, flag, 0.0)

    midpoint, factor_one, factor_two = coefficients(0)

    def fine_residuals(block, start, count):
        results = []
        for index, (total, middle) in enumerate(weighted(block, start + 1, count, True)):
            applied = (8.0 / 7.0 + reaction[start + index]) * middle - total * (1.0 / 56.0)
            results.append((refined * (source[start + index] - applied), middle))
        return results

    def add_edges(block, shares):
        (low, high), ends = shares
        for plane in range(planes):
            block[plane + 1, 8:16, :] += edge_tile(low, plane, False)
            block[plane + 1, rows : 8 + rows, :] += edge_tile(high, plane, True)
        block[1, 8 : 8 + rows, :] += ends[0]
        block[planes, 8 : 8 + rows, :] += ends[1]

    def first(start):
        for index, (residual, middle) in enumerate(fine_residuals(field_a, start, 8)):
            field_b[start + index + 1, 8 : 8 + rows, :] = middle + residual * (1.0 / midpoint)

    groups(0, planes, 8, first)
    add_edges(field_b, halo_a.finish(refined, 1.0 / (56.0 * midpoint)))
    halo_b.start()

    for plane in range(two):
        put(
            flat_one, plane, one,
            k_one[2 + 2 * plane, 8 : 8 + one, :] + k_one[3 + 2 * plane, 8 : 8 + one, :],
        )
    spread(flat_one, k_two, two, 1)
    for plane in range(three):
        put(
            flat_two, plane, two,
            k_two[2 + 2 * plane, 8 : 8 + two, :] + k_two[3 + 2 * plane, 8 : 8 + two, :],
        )
    small = paired(flat_two, matrices.at[2])
    halo_k.start(small[0:8] + roll(small[8:16], 64, 1))

    def second(start):
        for index, (residual, middle) in enumerate(fine_residuals(field_b, start, 8)):
            before = field_a[start + index + 1, 8 : 8 + rows, :]
            step = factor_one * (middle - before) + factor_two * residual
            field_c[start + index + 1, 8 : 8 + rows, :] = middle + step

    groups(0, planes, 8, second)
    halo_a.drain()
    add_edges(field_c, halo_b.finish(refined, factor_two / 56.0))
    halo_c.start()
    stores[0].start()

    def third(start):
        values = fine_residuals(field_c, 2 * start, 8)
        for index in range(4):
            put(flat_zero, start + index, rows, values[2 * index][0] + values[2 * index + 1][0])

    groups(0, one, 4, third)
    halo_b.drain()
    (low, high), ends = halo_c.finish(refined, 1.0 / 56.0)
    for plane in range(one):
        at = plane * rows
        for strip, last, begin in ((low, False, at), (high, True, at + rows - 8)):
            both = edge_tile(strip, 2 * plane, last) + edge_tile(strip, 2 * plane + 1, last)
            flat_zero[begin : begin + 8, :] += both
    flat_zero[0:rows, :] += ends[0]
    flat_zero[(one - 1) * rows : one * rows, :] += ends[1]
    spread(flat_zero, f_one, one, 0)
    halo_f_one.start()

    halo_k.finish(k_three)
    for plane in range(6):
        flat_extra[16 * plane : 16 * plane + 16, :] = k_three[2 * plane] + k_three[2 * plane + 1]
    k_four[...] = paired(flat_extra, matrices.at[3]).reshape(6, 8, 128)
    halo_c.drain()
    halo_k.drain()

    def correct(level, f, k, e, start, count, mask):
        midpoint, factor_one, factor_two = coefficients(level)
        slope = factor_two / midpoint
        keep = (1.0 + factor_one) / midpoint + factor_two - slope * 8.0 / 7.0
        for index, (total, middle) in enumerate(weighted(f, start, count, False)):
            plane = start + index
            value = (keep - slope * k[plane]) * middle + (slope / 56.0) * total
            e[plane] = value * mask(plane)

    def left_over(f, k, e, start, count):
        return [
            f[start + index]
            - ((8.0 / 7.0 + k[start + index]) * middle - total * (1.0 / 56.0))
            for index, (total, middle) in enumerate(weighted(e, start, count, False))
        ]

    for level, f, k, e, exchange, held, flat, size, spans in (
        (1, f_one, k_one, e_one, halo_f_one, held_one, flat_one, one, (6, 4)),
        (2, f_two, k_two, e_two, halo_f_two, held_two, flat_two, two, (10, 4)),
    ):
        extent = depth >> level
        exchange.finish()
        row_mask = in_grid(
            8 - place.agg * size, 8 + (counts[1] - place.agg) * size, f.shape[1:], extent
        )

        def mask(plane, size=size, row_mask=row_mask):
            return row_mask * plane_in_grid(place.box * size + plane - 2, counts[0] * size)

        def ahead(start, level=level, f=f, k=k, e=e, span=spans[0], mask=mask):
            correct(level, f, k, e, start, span, mask)

        groups(1, size + 2, spans[0], ahead)

        def remainder(start, f=f, k=k, e=e, size=size, flat=flat, span=spans[1]):
            values = left_over(f, k, e, 2 * start + 2, 2 * span)
            for index in range(span):
                total = values[2 * index] + values[2 * index + 1]
                put(flat, start + index, size, total[8 : 8 + size])

        groups(0, size // 2, spans[1], remainder)
        if level == 1:
            spread(flat, f_two, size // 2, level)
            halo_f_two.start()
        else:
            small = paired(flat, matrices.at[level])
            tiles_three[1, 1] = small[0:8] + roll(small[8:16], 64, 1)
            gather_three.start()
        held[...] = e[2 : 2 + size, 8 : 8 + size, 0:extent]
        stores[level].start()
        exchange.drain()

    mask_three = in_grid(
        4 - place.agg * three, 4 + (counts[1] - place.agg) * three, f_three.shape[1:], depth // 8
    )

    def at_three(plane):
        return mask_three * plane_in_grid(place.box * three + plane - 4, counts[0] * three)

    gather_three.arrive()
    lay_out([[tiles_three[bx, by] for by in range(3)] for bx in range(3)], f_three)
    correct(3, f_three, k_three, e_three, 3, 6, at_three)
    values = left_over(f_three, k_three, e_three, 4, 4)
    for plane in range(2):
        flat_three[16 * plane : 16 * plane + 16, :] = values[2 * plane] + values[2 * plane + 1]
    tiles_four[1, 1] = paired(flat_three, matrices.at[3]).reshape(2, 8, 128)
    gather_four.start()
    held_three[...] = e_three[4:8, 4:8, 0 : depth // 8]
    stores[3].start()
    gather_three.drain()

    four = three // 2
    mask_four = in_grid(
        2 - place.agg * four, 2 + (counts[1] - place.agg) * four, f_four.shape[1:], depth // 16
    )

    def at_four(plane):
        return mask_four * plane_in_grid(place.box * four + plane - 2, counts[0] * four)

    gather_four.arrive()
    ids = row_ids((8, 128))
    for plane in range(6):
        before, own, after = (tiles_four[plane // 2, by, plane % 2] for by in range(3))
        value = jnp.where(ids < 4, own, roll(after, 2, 0))
        value = jnp.where(ids < 2, roll(before, -2, 0), value)
        f_four[plane] = jnp.where(ids < 6, value, 0.0)
    correct(4, f_four, k_four, e_four, 1, 4, at_four)
    held_four[...] = e_four[2:4, 2:4, 0 : depth // 16]
    stores[4].start()
    for index, value in enumerate(left_over(f_four, k_four, e_four, 2, 2)):
        held_bottom[index] = value[2:4, 0 : depth // 16]
    stores[5].start()
    gather_four.drain()
    for store in stores:
        store.wait()


def hand_on(*refs):
    sources, targets, held = refs[0:6], refs[6:12], refs[12:18]
    semaphores = refs[18]
    size = sources[0].shape[0] // 4
    parts = [(0, pl.ds(piece * size, size)) for piece in range(4)]
    parts += [(index, pl.ds(0, sources[index].shape[0])) for index in range(1, 6)]
    inward, outward = [], []
    for number, (index, part) in enumerate(parts):
        inner = held[index].at[part]
        inward.append(
            pltpu.make_async_copy(sources[index].at[part], inner, semaphores.at[0, number])
        )
        outward.append(
            pltpu.make_async_copy(inner, targets[index].at[part], semaphores.at[1, number])
        )
    for copy in inward:
        copy.start()
    for before, after in zip(inward, outward):
        before.wait()
        after.start()
    for copy in outward:
        copy.wait()


def per_device(counts, source, guess, reaction, flags):
    planes, rows, depth = source.shape
    assert planes == rows and planes == 32 and depth == 128 and flags.shape[:2] == (1, 1)
    f32 = jnp.float32

    def vmem(*shape):
        return pltpu.VMEM(shape, f32)

    one, two = planes // 2, planes // 4
    scratch = [pltpu.VMEM(flags.shape, jnp.int32)] + [vmem(planes, rows, depth)] * 2
    scratch += [vmem(planes + 2, rows + 16, depth)] * 3 + [vmem(3, 2, rows + 16, depth)]
    scratch += [pltpu.VMEM((LEVELS, 256, 128), jnp.bfloat16)]
    scratch += [vmem(one + 4, one + 16, 128)] * 3 + [vmem(two + 4, two + 16, 128)] * 3
    scratch += [vmem(12, 16, 128)] * 3 + [vmem(6, 8, 128)] * 3
    scratch += [vmem(one * rows, 128), vmem(two * one, 128), vmem(two // 2 * two, 128)]
    scratch += [vmem(32, 128), vmem(96, 128)]
    scratch += [vmem(3, 2, planes // 8, 8, 128)] * 2
    scratch += [vmem(1, 2, one // 8, 8, 128)] * 2 + [vmem(1, 2, two // 8, 8, 128)] * 2
    k_tiles = one // 8 + two // 8 + 1
    k_planes = 2 * (one // 8 + two // 8) + 1
    scratch += [vmem(5, 4, 8, 128), vmem(2, k_tiles, 8, 128), vmem(2, k_planes, 8, 128)]
    scratch += [vmem(2, k_tiles, 8, 128), vmem(4, k_tiles, 8, 128), vmem(2, k_planes, 8, 128)]
    scratch += [vmem(3, 3, 8, 128), vmem(3, 3, 2, 8, 128)]
    outs = [jax.ShapeDtypeStruct(source.shape, f32)]
    for level in range(1, LEVELS + 1):
        outs.append(
            jax.ShapeDtypeStruct((planes >> level, rows >> level, depth >> level), f32)
        )
    outs.append(outs[-1])
    scratch += [vmem(*out.shape) for out in outs[1:]]
    scratch += [pltpu.SemaphoreType.DMA((8, 8))] * 2
    scratch += [pltpu.SemaphoreType.DMA((19,))]
    anywhere = pl.BlockSpec(memory_space=pl.ANY)
    results = pl.pallas_call(
        functools.partial(kernel, counts),
        out_shape=outs,
        in_specs=[anywhere] * 4,
        out_specs=[anywhere] * 6,
        scratch_shapes=scratch,
        compiler_params=pltpu.CompilerParams(
            collective_id=0, has_side_effects=True, vmem_limit_bytes=60 * 1024 * 1024
        ),
    )(flags, source, guess, reaction)
    return tuple(
        pl.pallas_call(
            hand_on,
            out_shape=outs,
            in_specs=[anywhere] * 6,
            out_specs=[anywhere] * 6,
            scratch_shapes=[vmem(*out.shape) for out in outs] + [pltpu.SemaphoreType.DMA((2, 9))],
            compiler_params=pltpu.CompilerParams(vmem_limit_bytes=60 * 1024 * 1024),
        )(*results)
    )


def solution(mesh):
    spec = P("box", "agg", None)
    counts = (mesh.shape["box"], mesh.shape["agg"])
    return jax.shard_map(
        functools.partial(per_device, counts),
        mesh=mesh,
        in_specs=(spec,) * 4,
        out_specs=(spec,) * 6,
        check_vma=False,
    )
```

```python
import functools

import jax
import jax.numpy as jnp
from jax import lax
from jax.experimental import pallas as pl
from jax.experimental.pallas import tpu as pltpu
from jax.sharding import PartitionSpec as P

LEVELS = 4
MESH = pl.DeviceIdType.MESH
NEAR = [(dx, dy) for dx in (-1, 0, 1) for dy in (-1, 0, 1) if (dx, dy) != (0, 0)]


def coefficients(level_index):
    upper_edge = 1.1 * (2.0 + 0.02 * 4.0**level_index)
    lower_edge = upper_edge / 8.0
    midpoint = (upper_edge + lower_edge) / 2.0
    half_span = (upper_edge - lower_edge) / 2.0
    sigma_value = midpoint / half_span
    rho_first = 1.0 / sigma_value
    rho_second = 1.0 / (2.0 * sigma_value - rho_first)
    return (midpoint, rho_second * rho_first, 2.0 * rho_second / half_span)


def row_ids(shape):
    return lax.broadcasted_iota(jnp.int32, shape, len(shape) - 2)


def lane_ids(shape):
    return lax.broadcasted_iota(jnp.int32, shape, len(shape) - 1)


def roll(value, shift, dim):
    size = value.shape[dim]
    shift = shift % size
    return value if shift == 0 else pltpu.roll(value, shift, dim)


def slot_place(slot, width):
    if width == 1:
        return slot, 0
    return 2 * (slot % 4), slot // 4


def slot_mask(slot, width):
    row, half = slot_place(slot, width)
    rows, lanes = row_ids((8, 128)), lane_ids((8, 128))
    mask = (rows >= row) & (rows < row + width)
    if width > 1:
        mask = mask & ((lanes >= 64) if half else (lanes < 64))
    return mask


def unpacked(tile, slot, width, low):
    row, half = slot_place(slot, width)
    rows, lanes = row_ids((8, 128)), lane_ids((8, 128))
    value = roll(tile, (8 - width if low else 0) - row, 0)
    if half:
        value = roll(value, 64, 1)
    mask = (rows >= 8 - width) if low else (rows < width)
    if width > 1:
        mask = mask & (lanes < 64)
    return jnp.where(mask, value, 0.0)


def pack_edges(block, width, high, low):
    planes, rows = block.shape[0] - 2 * width, block.shape[1] - 16
    for tile in range(planes // 8):
        upper = jnp.zeros((8, 128), jnp.float32)
        lower = upper
        for slot in range(8):
            row, half = slot_place(slot, width)
            mask = slot_mask(slot, width)
            plane = width + 8 * tile + slot
            last = roll(block[plane, rows : rows + 8, :], row + width - 8, 0)
            first = roll(block[plane, 8:16, :], row, 0)
            if half:
                last, first = roll(last, 64, 1), roll(first, 64, 1)
            upper = jnp.where(mask, last, upper)
            lower = jnp.where(mask, first, lower)
        high[tile] = upper
        low[tile] = lower


def unpack_edges(block, width, tile, low, high):
    rows = block.shape[1] - 16
    for slot in range(8):
        plane = width + 8 * tile + slot
        block[plane, 0:8, :] = unpacked(low, slot, width, True)
        block[plane, rows + 8 : rows + 16, :] = unpacked(high, slot, width, False)


def unpack_corners(block, width, side, low, high):
    planes, rows = block.shape[0] - 2 * width, block.shape[1] - 16
    for index in range(width):
        slot = 8 - width + index if side == 0 else index
        plane = index if side == 0 else planes + width + index
        block[plane, 0:8, :] = unpacked(low, slot, width, True)
        block[plane, rows + 8 : rows + 16, :] = unpacked(high, slot, width, False)


class Halo:
    def __init__(self, place, block, width, packs, sides, corners, send, recv):
        self.place, self.block, self.width = place, block, width
        self.packs, self.sides, self.corners = packs, sides, corners
        self.send, self.recv = send, recv
        self.planes = block.shape[0] - 2 * width
        self.rows = block.shape[1] - 16

    def clear(self):
        w, planes = self.width, self.planes
        edge = jnp.zeros((w,) + self.block.shape[1:], jnp.float32)
        self.block[0:w] = edge
        self.block[planes + w : planes + 2 * w] = edge
        self.sides[...] = jnp.zeros(self.sides.shape, jnp.float32)
        self.corners[...] = jnp.zeros(self.corners.shape, jnp.float32)

    def copy(self, number):
        dx, dy = NEAR[number]
        w, planes, rows, block = self.width, self.planes, self.rows, self.block
        if dy == 0:
            source = block.at[planes : planes + w] if dx > 0 else block.at[w : 2 * w]
            target = block.at[0:w] if dx > 0 else block.at[planes + w : planes + 2 * w]
            source, target = source.at[:, 8 : 8 + rows], target.at[:, 8 : 8 + rows]
        else:
            pack = self.packs.at[0 if dy > 0 else 1]
            if dx == 0:
                source, target = pack, self.sides.at[0 if dy > 0 else 1]
            else:
                source = pack.at[planes // 8 - 1 if dx > 0 else 0]
                target = self.corners.at[(0 if dx > 0 else 2) + (0 if dy > 0 else 1)]
        return pltpu.make_async_remote_copy(
            src_ref=source,
            dst_ref=target,
            send_sem=self.send.at[number],
            recv_sem=self.recv.at[number],
            device_id=self.place.device(dx, dy),
            device_id_type=MESH,
        )

    def start(self):
        for number, (dx, dy) in enumerate(NEAR):
            if dy == 0:
                pl.when(self.place.has(dx, dy))(lambda n=number: self.copy(n).start())
        pack_edges(self.block, self.width, self.packs.at[0], self.packs.at[1])
        for number, (dx, dy) in enumerate(NEAR):
            if dy != 0:
                pl.when(self.place.has(dx, dy))(lambda n=number: self.copy(n).start())

    def finish(self):
        self.arrive()
        for tile in range(self.planes // 8):
            unpack_edges(self.block, self.width, tile, self.sides[0, tile], self.sides[1, tile])
        for side in (0, 1):
            low, high = self.corners[2 * side], self.corners[2 * side + 1]
            unpack_corners(self.block, self.width, side, low, high)

    def arrive(self):
        for number, (dx, dy) in enumerate(NEAR):
            pl.when(self.place.has(-dx, -dy))(lambda n=number: self.copy(n).wait_recv())

    def drain(self):
        for number, (dx, dy) in enumerate(NEAR):
            pl.when(self.place.has(dx, dy))(lambda n=number: self.copy(n).wait_send())


class FineHalo(Halo):
    def __init__(self, place, block, packs, sides, corners, outer, send, recv):
        super().__init__(place, block, 1, packs, sides, corners, send, recv)
        self.outer = outer

    def clear(self):
        planes, rows = self.planes, self.rows
        edge = jnp.zeros((1,) + self.block.shape[1:], jnp.float32)
        self.block[0:1] = edge
        self.block[planes + 1 : planes + 2] = edge
        strip = jnp.zeros((planes + 2, 8, 128), jnp.float32)
        self.block[:, 0:8, :] = strip
        self.block[:, 8 + rows : 16 + rows, :] = strip
        for ref in (self.sides, self.corners, self.outer):
            ref[...] = jnp.zeros(ref.shape, jnp.float32)

    def copy(self, number):
        dx, dy = NEAR[number]
        if dy != 0:
            return super().copy(number)
        plane = self.planes if dx > 0 else 1
        return pltpu.make_async_remote_copy(
            src_ref=self.block.at[plane, 8 : 8 + self.rows],
            dst_ref=self.outer.at[0 if dx > 0 else 1, 8 : 8 + self.rows],
            send_sem=self.send.at[number],
            recv_sem=self.recv.at[number],
            device_id=self.place.device(dx, dy),
            device_id_type=MESH,
        )

    def finish(self, refined, scale):
        planes, rows = self.planes, self.rows
        for number, (dx, dy) in enumerate(NEAR):
            pl.when(self.place.has(-dx, -dy))(lambda n=number: self.copy(n).wait_recv())
        factor = refined * scale
        sides, ends = [], []
        for side in (0, 1):
            strip = self.sides[side].reshape(planes, 128)
            at = row_ids(strip.shape)
            before = jnp.where(at == 0, 0.0, roll(strip, 1, 0))
            after = jnp.where(at == planes - 1, 0.0, roll(strip, -1, 0))
            sides.append(factor * along_lanes((before + after) + (strip + strip), True))
        for end in (0, 1):
            slot = 7 if end == 0 else 0
            low, high = self.corners[2 * end], self.corners[2 * end + 1]
            plane = jnp.concatenate(
                [
                    unpacked(low, slot, 1, True),
                    self.outer[end, 8 : 8 + rows, :],
                    unpacked(high, slot, 1, False),
                ],
                axis=0,
            )
            total = (roll(plane, 1, 0) + roll(plane, -1, 0)) + (plane + plane)
            ends.append(factor * along_lanes(total[8 : 8 + rows], True))
        return sides, ends


def edge_tile(strip, plane, last):
    base = plane // 8 * 8
    value = roll(strip[base : base + 8], (7 if last else 0) - plane % 8, 0)
    return jnp.where(row_ids((8, 128)) == (7 if last else 0), value, 0.0)


class Coefficients(Halo):
    def __init__(self, place, fields, packs, ends, sides, corners, outer, send, recv):
        self.place, self.fields = place, fields
        self.packs, self.ends = packs, ends
        self.sides, self.corners, self.outer = sides, corners, outer
        self.send, self.recv = send, recv

    def clear(self):
        for ref in (self.sides, self.corners, self.outer):
            ref[...] = jnp.zeros(ref.shape, jnp.float32)

    def copy(self, number):
        dx, dy = NEAR[number]
        across, along = (0 if dx > 0 else 1), (0 if dy > 0 else 1)
        if dy == 0:
            source, target = self.ends.at[across], self.outer.at[across]
        else:
            source = self.packs.at[along]
            target = self.sides.at[along] if dx == 0 else self.corners.at[2 * across + along]
        return pltpu.make_async_remote_copy(
            src_ref=source,
            dst_ref=target,
            send_sem=self.send.at[number],
            recv_sem=self.recv.at[number],
            device_id=self.place.device(dx, dy),
            device_id_type=MESH,
        )

    def start(self, tiles):
        self.tiles = tiles
        at = 0
        for block in self.fields:
            size = (block.shape[0] - 4) // 8
            part = pl.ds(at, size)
            pack_edges(block, 2, self.packs.at[0, part], self.packs.at[1, part])
            at += size
        at = 0
        for block in self.fields:
            planes, rows = block.shape[0] - 4, block.shape[1] - 16
            size = rows // 8
            for index in range(2):
                for across, plane in ((0, planes + index), (1, 2 + index)):
                    value = block[plane, 8 : 8 + rows, :].reshape(size, 8, 128)
                    self.ends[across, at : at + size] = value
                at += size
        for ref in (self.packs, self.ends):
            for index in range(2):
                for where, tile in enumerate(tiles):
                    ref[index, ref.shape[1] - 2 + where] = tile
        for number, (dx, dy) in enumerate(NEAR):
            pl.when(self.place.has(dx, dy))(lambda n=number: self.copy(n).start())

    def finish(self, second):
        self.arrive()
        at, end = 0, 0
        for block in self.fields:
            planes, rows = block.shape[0] - 4, block.shape[1] - 16
            count, size = planes // 8, rows // 8
            for tile in range(count):
                low, high = self.sides[0, at + tile], self.sides[1, at + tile]
                unpack_edges(block, 2, tile, low, high)
            for side in (0, 1):
                tile = at + (count - 1 if side == 0 else 0)
                low, high = self.corners[2 * side, tile], self.corners[2 * side + 1, tile]
                unpack_corners(block, 2, side, low, high)
                for index in range(2):
                    plane = index if side == 0 else planes + 2 + index
                    first = end + index * size
                    value = self.outer[side, first : first + size].reshape(rows, 128)
                    block[plane, 8 : 8 + rows, :] = value
            at += count
            end += 2 * size
        around = []
        for part in range(2):
            side, last = at + part, end + part
            around.append(
                [
                    [self.corners[0, side], self.outer[0, last], self.corners[1, side]],
                    [self.sides[0, side], self.tiles[part], self.sides[1, side]],
                    [self.corners[2, side], self.outer[1, last], self.corners[3, side]],
                ]
            )
        lay_out(around, second)


def fold(values):
    tiles = []
    for part in range(2):
        planes = [roll(values[32 * part + 8 * at : 32 * part + 8 * at + 8], 32 * at, 1) for at in range(4)]
        tiles.append((planes[0] + planes[1]) + (planes[2] + planes[3]))
    return tiles


def lay_out(around, field):
    lanes = lane_ids((8, 128))
    for bx in range(3):
        for by in range(3):
            for index in range(8):
                value = roll(around[index // 4][bx][by], -32 * (index % 4), 1)
                value = jnp.where(lanes < 32, value, 0.0)
                field[8 * bx + index, 8 * by : 8 * by + 8, :] = value


class Gather(Halo):
    def __init__(self, place, tiles, send, recv):
        self.place, self.tiles, self.send, self.recv = place, tiles, send, recv

    def clear(self):
        self.tiles[...] = jnp.zeros(self.tiles.shape, jnp.float32)

    def copy(self, number):
        dx, dy = NEAR[number]
        return pltpu.make_async_remote_copy(
            src_ref=self.tiles.at[1, 1],
            dst_ref=self.tiles.at[1 - dx, 1 - dy],
            send_sem=self.send.at[number],
            recv_sem=self.recv.at[number],
            device_id=self.place.device(dx, dy),
            device_id_type=MESH,
        )

    def start(self):
        for number, (dx, dy) in enumerate(NEAR):
            pl.when(self.place.has(dx, dy))(lambda n=number: self.copy(n).start())


class Place:
    def __init__(self, counts):
        self.counts = counts
        self.box, self.agg = lax.axis_index("box"), lax.axis_index("agg")

    def device(self, dx, dy):
        return (self.box + dx, self.agg + dy)

    def has(self, dx, dy):
        x, y = self.device(dx, dy)
        return (x >= 0) & (x < self.counts[0]) & (y >= 0) & (y < self.counts[1])

    def greet(self):
        semaphore = pltpu.get_barrier_semaphore()
        for dx, dy in NEAR:

            @pl.when(self.has(dx, dy))
            def _(dx=dx, dy=dy):
                pl.semaphore_signal(
                    semaphore, inc=1, device_id=self.device(dx, dy), device_id_type=MESH
                )

    def await_greetings(self):
        spans = []
        for at, count in zip((self.box, self.agg), self.counts):
            spans.append(1 + jnp.minimum(at, 1) + jnp.minimum(count - 1 - at, 1))
        pl.semaphore_wait(pltpu.get_barrier_semaphore(), spans[0] * spans[1] - 1)


def along_lanes(total, wrap):
    left, right = roll(total, 1, 1), roll(total, -1, 1)
    if wrap:
        lanes = lane_ids(total.shape)
        left = jnp.where(lanes == 0, 0.0, left)
        right = jnp.where(lanes == 127, 0.0, right)
    return (left + right) + (total + total)


def weighted(block, start, count, wrap):
    held = [block[start - 1 + index] for index in range(count + 2)]
    pairs = [low + high for low, high in zip(held[:-1], held[1:])]
    results = []
    for index in range(count):
        total = pairs[index] + pairs[index + 1]
        total = (roll(total, 1, 0) + roll(total, -1, 0)) + (total + total)
        middle = held[index + 1]
        if wrap:
            total, middle = total[8:-8], middle[8:-8]
        results.append((along_lanes(total, wrap), middle))
    return results


def pair_matrix(extent):
    source, target = row_ids((256, 128)) % 128, lane_ids((256, 128))
    pairs = (source < extent) & ((source == 2 * target) | (source == 2 * target + 1))
    return jnp.where(pairs, 0.5, 0.0).astype(jnp.bfloat16)


def paired(flat, matrix):
    half = flat.shape[0] // 2
    rows = flat[pl.ds(0, half, stride=2), :] + flat[pl.ds(1, half, stride=2), :]
    high = rows.astype(jnp.bfloat16)
    low = (rows - high.astype(jnp.float32)).astype(jnp.bfloat16)
    return jnp.dot(
        jnp.concatenate([high, low], axis=1),
        matrix[...],
        preferred_element_type=jnp.float32,
    )


def in_grid(start, stop, shape, extent):
    rows, lanes = row_ids(shape), lane_ids(shape)
    return jnp.where((rows >= start) & (rows < stop) & (lanes < extent), 1.0, 0.0)


def plane_in_grid(index, count):
    return jnp.where((index >= 0) & (index < count), 1.0, 0.0)


def groups(start, count, size, body):
    assert count % size == 0
    if count == size:
        body(start)
        return

    def step(index, _):
        body(start + index * size)
        return 0

    lax.fori_loop(0, count // size, step, 0)


def kernel(
    counts,
    flags_in, source_in, guess_in, reaction_in,
    iterate, out_one, out_two, out_three, out_four, out_bottom,
    flags, source, reaction,
    field_a, field_b, field_c, outer, matrices,
    f_one, k_one, e_one, f_two, k_two, e_two,
    f_three, k_three, e_three, f_four, k_four, e_four,
    flat_zero, flat_one, flat_two, flat_three, flat_extra,
    packs_zero, sides_zero, packs_one, sides_one, corners,
    k_packs, k_ends, k_sides, k_corners, k_outer, tiles_two, tiles_four, held_one, held_two, held_three, held_four, held_bottom,
    near_send, near_recv, local,
):
    place = Place(counts)
    planes, rows, depth = source.shape

    def halo(number, block, width, packs, sides, index):
        return Halo(
            place, block, width, packs.at[index], sides.at[index], corners.at[number],
            near_send.at[number], near_recv.at[number],
        )

    halo_a, halo_b, halo_c = (
        FineHalo(
            place, block, packs_zero.at[index], sides_zero.at[index], corners.at[index],
            outer.at[index], near_send.at[index], near_recv.at[index],
        )
        for index, block in enumerate((field_a, field_b, field_c))
    )
    halo_f_one = halo(3, f_one, 2, packs_one, sides_one, 0)
    gather_two = Gather(place, tiles_two, near_send.at[4], near_recv.at[4])
    halo_k = Coefficients(
        place, (k_one,), k_packs, k_ends, k_sides, k_corners, k_outer,
        near_send.at[5], near_recv.at[5],
    )
    gather_four = Gather(place, tiles_four, near_send.at[6], near_recv.at[6])
    own_a = field_a.at[1 : 1 + planes, 8 : 8 + rows]
    own_c = field_c.at[1 : 1 + planes, 8 : 8 + rows]
    quarter = planes // 4
    parts = [pl.ds(index * quarter, quarter) for index in range(4)]
    pairs = [(guess_in.at[part], own_a.at[part]) for part in parts]
    pairs += [(flags_in, flags)]
    pairs += [(reaction_in.at[part], reaction.at[part]) for part in parts]
    pairs += [(source_in.at[part], source.at[part]) for part in parts]
    loads = [
        pltpu.make_async_copy(origin, target, local.at[6 + index])
        for index, (origin, target) in enumerate(pairs)
    ]
    stores = [
        pltpu.make_async_copy(origin, target, local.at[index])
        for index, (origin, target) in enumerate(
            (
                (own_c, iterate), (held_one, out_one), (held_two, out_two),
                (held_three, out_three), (held_four, out_four), (held_bottom, out_bottom),
            )
        )
    ]
    for load in loads[:4]:
        load.start()
    for exchange in (
        halo_a, halo_b, halo_c, halo_f_one, gather_two, halo_k, gather_four,
    ):
        exchange.clear()
    place.greet()
    flat_two[...] = jnp.zeros(flat_two.shape, jnp.float32)
    flat_extra[...] = jnp.zeros(flat_extra.shape, jnp.float32)
    for load in loads[4:]:
        load.start()
    for level in range(LEVELS):
        matrices[level] = pair_matrix(depth >> level)
    for load in loads[:4]:
        load.wait()
    place.await_greetings()
    halo_a.start()

    def spread(flat, target, count, level):
        values = paired(flat, matrices.at[level])
        target[2 : 2 + count, 8 : 8 + count, :] = values.reshape(count, count, 128)

    def put(flat, plane, size, value):
        flat[pl.ds(pl.multiple_of(plane * size, size), size), :] = value

    one, two, three = planes // 2, planes // 4, planes // 8
    for load in loads[4:9]:
        load.wait()

    def coarse_reaction(start):
        for plane in range(4):
            at = start + plane
            put(flat_zero, at, rows, reaction[2 * at] + reaction[2 * at + 1])

    groups(0, one, 4, coarse_reaction)
    spread(flat_zero, k_one, one, 0)
    for load in loads[9:]:
        load.wait()

    lanes = lane_ids((1, depth))
    patch = depth // flags.shape[2]
    refined = jnp.zeros((1, depth), jnp.float32)
    for box in range(flags.shape[2]):
        chosen = (lanes >= box * patch) & (lanes < (box + 1) * patch)
        flag = flags[0, :, box : box + 1].astype(jnp.float32)
        refined = refined + jnp.where(chosen, flag, 0.0)

    midpoint, factor_one, factor_two = coefficients(0)

    def fine_residuals(block, start, count):
        results = []
        for index, (total, middle) in enumerate(weighted(block, start + 1, count, True)):
            applied = (8.0 / 7.0 + reaction[start + index]) * middle - total * (1.0 / 56.0)
            results.append((refined * (source[start + index] - applied), middle))
        return results

    def add_edges(block, shares):
        (low, high), ends = shares
        for plane in range(planes):
            block[plane + 1, 8:16, :] += edge_tile(low, plane, False)
            block[plane + 1, rows : 8 + rows, :] += edge_tile(high, plane, True)
        block[1, 8 : 8 + rows, :] += ends[0]
        block[planes, 8 : 8 + rows, :] += ends[1]

    def first(start):
        for index, (residual, middle) in enumerate(fine_residuals(field_a, start, 8)):
            field_b[start + index + 1, 8 : 8 + rows, :] = middle + residual * (1.0 / midpoint)

    groups(0, planes, 8, first)
    add_edges(field_b, halo_a.finish(refined, 1.0 / (56.0 * midpoint)))
    halo_b.start()

    for plane in range(two):
        put(
            flat_one, plane, one,
            k_one[2 + 2 * plane, 8 : 8 + one, :] + k_one[3 + 2 * plane, 8 : 8 + one, :],
        )
    k_tiles = fold(paired(flat_one, matrices.at[1]))
    halo_k.start(k_tiles)

    def second(start):
        for index, (residual, middle) in enumerate(fine_residuals(field_b, start, 8)):
            before = field_a[start + index + 1, 8 : 8 + rows, :]
            step = factor_one * (middle - before) + factor_two * residual
            field_c[start + index + 1, 8 : 8 + rows, :] = middle + step

    groups(0, planes, 8, second)
    halo_a.drain()
    add_edges(field_c, halo_b.finish(refined, factor_two / 56.0))
    halo_c.start()
    stores[0].start()

    def third(start):
        values = fine_residuals(field_c, 2 * start, 8)
        for index in range(4):
            put(flat_zero, start + index, rows, values[2 * index][0] + values[2 * index + 1][0])

    groups(0, one, 4, third)
    halo_b.drain()
    (low, high), ends = halo_c.finish(refined, 1.0 / 56.0)
    for plane in range(one):
        at = plane * rows
        for strip, last, begin in ((low, False, at), (high, True, at + rows - 8)):
            both = edge_tile(strip, 2 * plane, last) + edge_tile(strip, 2 * plane + 1, last)
            flat_zero[begin : begin + 8, :] += both
    flat_zero[0:rows, :] += ends[0]
    flat_zero[(one - 1) * rows : one * rows, :] += ends[1]
    spread(flat_zero, f_one, one, 0)
    halo_f_one.start()

    halo_k.finish(k_two)
    for plane in range(12):
        flat_extra[32 * plane : 32 * plane + 24, :] = k_two[2 * plane] + k_two[2 * plane + 1]
    k_three[...] = paired(flat_extra, matrices.at[2]).reshape(12, 16, 128)
    for plane in range(6):
        flat_three[16 * plane : 16 * plane + 16, :] = k_three[2 * plane] + k_three[2 * plane + 1]
    k_four[...] = paired(flat_three, matrices.at[3]).reshape(6, 8, 128)
    halo_c.drain()
    halo_k.drain()

    def correct(level, f, k, e, start, count, mask):
        midpoint, factor_one, factor_two = coefficients(level)
        slope = factor_two / midpoint
        keep = (1.0 + factor_one) / midpoint + factor_two - slope * 8.0 / 7.0
        for index, (total, middle) in enumerate(weighted(f, start, count, False)):
            plane = start + index
            value = (keep - slope * k[plane]) * middle + (slope / 56.0) * total
            e[plane] = value * mask(plane)

    def left_over(f, k, e, start, count):
        return [
            f[start + index]
            - ((8.0 / 7.0 + k[start + index]) * middle - total * (1.0 / 56.0))
            for index, (total, middle) in enumerate(weighted(e, start, count, False))
        ]

    halo_f_one.finish()
    mask_one = in_grid(
        8 - place.agg * one, 8 + (counts[1] - place.agg) * one, f_one.shape[1:], depth // 2
    )

    def at_one(plane):
        return mask_one * plane_in_grid(place.box * one + plane - 2, counts[0] * one)

    groups(1, one + 2, 6, lambda start: correct(1, f_one, k_one, e_one, start, 6, at_one))

    def remainder(start):
        values = left_over(f_one, k_one, e_one, 2 * start + 2, 8)
        for index in range(4):
            total = values[2 * index] + values[2 * index + 1]
            put(flat_one, start + index, one, total[8 : 8 + one])

    groups(0, two, 4, remainder)
    for part, tile in enumerate(fold(paired(flat_one, matrices.at[1]))):
        tiles_two[1, 1, part] = tile
    gather_two.start()
    held_one[...] = e_one[2 : 2 + one, 8 : 8 + one, 0 : depth // 2]
    stores[1].start()
    halo_f_one.drain()

    mask_two = in_grid(
        8 - place.agg * two, 8 + (counts[1] - place.agg) * two, f_two.shape[1:], depth // 4
    )

    def at_two(plane):
        return mask_two * plane_in_grid(place.box * two + plane - 8, counts[0] * two)

    gather_two.arrive()
    lay_out(
        [
            [[tiles_two[bx, by, part] for by in range(3)] for bx in range(3)]
            for part in range(2)
        ],
        f_two,
    )
    correct(2, f_two, k_two, e_two, 3, 18, at_two)
    values = left_over(f_two, k_two, e_two, 4, 16)
    for plane in range(8):
        total = values[2 * plane] * at_two(4 + 2 * plane)
        total = total + values[2 * plane + 1] * at_two(5 + 2 * plane)
        flat_two[32 * plane : 32 * plane + 24, :] = total
    f_three[2:10] = paired(flat_two, matrices.at[2]).reshape(8, 16, 128)

    mask_three = in_grid(
        4 - place.agg * three, 4 + (counts[1] - place.agg) * three, f_three.shape[1:], depth // 8
    )

    def at_three(plane):
        return mask_three * plane_in_grid(place.box * three + plane - 4, counts[0] * three)

    correct(3, f_three, k_three, e_three, 3, 6, at_three)
    values = left_over(f_three, k_three, e_three, 4, 4)
    for plane in range(2):
        flat_three[16 * plane : 16 * plane + 16, :] = values[2 * plane] + values[2 * plane + 1]
    tiles_four[1, 1] = paired(flat_three.at[0:32], matrices.at[3]).reshape(2, 8, 128)
    gather_four.start()
    held_three[...] = e_three[4:8, 4:8, 0 : depth // 8]
    stores[3].start()
    held_two[...] = e_two[8 : 8 + two, 8 : 8 + two, 0 : depth // 4]
    stores[2].start()
    gather_two.drain()

    four = three // 2
    mask_four = in_grid(
        2 - place.agg * four, 2 + (counts[1] - place.agg) * four, f_four.shape[1:], depth // 16
    )

    def at_four(plane):
        return mask_four * plane_in_grid(place.box * four + plane - 2, counts[0] * four)

    gather_four.arrive()
    ids = row_ids((8, 128))
    for plane in range(6):
        before, own, after = (tiles_four[plane // 2, by, plane % 2] for by in range(3))
        value = jnp.where(ids < 4, own, roll(after, 2, 0))
        value = jnp.where(ids < 2, roll(before, -2, 0), value)
        f_four[plane] = jnp.where(ids < 6, value, 0.0)
    correct(4, f_four, k_four, e_four, 1, 4, at_four)
    held_four[...] = e_four[2:4, 2:4, 0 : depth // 16]
    stores[4].start()
    for index, value in enumerate(left_over(f_four, k_four, e_four, 2, 2)):
        held_bottom[index] = value[2:4, 0 : depth // 16]
    stores[5].start()
    gather_four.drain()
    for store in stores:
        store.wait()


def hand_on(*refs):
    sources, targets, held = refs[0:6], refs[6:12], refs[12:18]
    semaphores = refs[18]
    size = sources[0].shape[0] // 4
    parts = [(0, pl.ds(piece * size, size)) for piece in range(4)]
    parts += [(index, pl.ds(0, sources[index].shape[0])) for index in range(1, 6)]
    inward, outward = [], []
    for number, (index, part) in enumerate(parts):
        inner = held[index].at[part]
        inward.append(
            pltpu.make_async_copy(sources[index].at[part], inner, semaphores.at[0, number])
        )
        outward.append(
            pltpu.make_async_copy(inner, targets[index].at[part], semaphores.at[1, number])
        )
    for copy in inward:
        copy.start()
    for before, after in zip(inward, outward):
        before.wait()
        after.start()
    for copy in outward:
        copy.wait()


def per_device(counts, source, guess, reaction, flags):
    planes, rows, depth = source.shape
    assert planes == rows and planes == 32 and depth == 128 and flags.shape[:2] == (1, 1)
    f32 = jnp.float32

    def vmem(*shape):
        return pltpu.VMEM(shape, f32)

    one, two = planes // 2, planes // 4
    scratch = [pltpu.VMEM(flags.shape, jnp.int32)] + [vmem(planes, rows, depth)] * 2
    scratch += [vmem(planes + 2, rows + 16, depth)] * 3 + [vmem(3, 2, rows + 16, depth)]
    scratch += [pltpu.VMEM((LEVELS, 256, 128), jnp.bfloat16)]
    scratch += [vmem(one + 4, one + 16, 128)] * 3 + [vmem(24, 24, 128)] * 3
    scratch += [vmem(12, 16, 128)] * 3 + [vmem(6, 8, 128)] * 3
    scratch += [vmem(one * rows, 128), vmem(two * one, 128), vmem(256, 128)]
    scratch += [vmem(96, 128), vmem(384, 128)]
    scratch += [vmem(3, 2, planes // 8, 8, 128)] * 2
    scratch += [vmem(1, 2, one // 8, 8, 128)] * 2
    k_tiles = one // 8 + 2
    k_planes = 2 * (one // 8) + 2
    scratch += [vmem(4, 4, 8, 128), vmem(2, k_tiles, 8, 128), vmem(2, k_planes, 8, 128)]
    scratch += [vmem(2, k_tiles, 8, 128), vmem(4, k_tiles, 8, 128), vmem(2, k_planes, 8, 128)]
    scratch += [vmem(3, 3, 2, 8, 128)] * 2
    outs = [jax.ShapeDtypeStruct(source.shape, f32)]
    for level in range(1, LEVELS + 1):
        outs.append(
            jax.ShapeDtypeStruct((planes >> level, rows >> level, depth >> level), f32)
        )
    outs.append(outs[-1])
    scratch += [vmem(*out.shape) for out in outs[1:]]
    scratch += [pltpu.SemaphoreType.DMA((7, 8))] * 2
    scratch += [pltpu.SemaphoreType.DMA((19,))]
    anywhere = pl.BlockSpec(memory_space=pl.ANY)
    results = pl.pallas_call(
        functools.partial(kernel, counts),
        out_shape=outs,
        in_specs=[anywhere] * 4,
        out_specs=[anywhere] * 6,
        scratch_shapes=scratch,
        compiler_params=pltpu.CompilerParams(
            collective_id=0, has_side_effects=True, vmem_limit_bytes=60 * 1024 * 1024
        ),
    )(flags, source, guess, reaction)
    return tuple(
        pl.pallas_call(
            hand_on,
            out_shape=outs,
            in_specs=[anywhere] * 6,
            out_specs=[anywhere] * 6,
            scratch_shapes=[vmem(*out.shape) for out in outs] + [pltpu.SemaphoreType.DMA((2, 9))],
            compiler_params=pltpu.CompilerParams(vmem_limit_bytes=60 * 1024 * 1024),
        )(*results)
    )


def solution(mesh):
    spec = P("box", "agg", None)
    counts = (mesh.shape["box"], mesh.shape["agg"])
    return jax.shard_map(
        functools.partial(per_device, counts),
        mesh=mesh,
        in_specs=(spec,) * 4,
        out_specs=(spec,) * 6,
        check_vma=False,
    )
```

```python
import functools

import jax
import jax.numpy as jnp
from jax import lax
from jax.experimental import pallas as pl
from jax.experimental.pallas import tpu as pltpu
from jax.sharding import PartitionSpec as P

LEVELS = 4
MESH = pl.DeviceIdType.MESH
NEAR = [(dx, dy) for dx in (-1, 0, 1) for dy in (-1, 0, 1) if (dx, dy) != (0, 0)]


def coefficients(level_index):
    upper_edge = 1.1 * (2.0 + 0.02 * 4.0**level_index)
    lower_edge = upper_edge / 8.0
    midpoint = (upper_edge + lower_edge) / 2.0
    half_span = (upper_edge - lower_edge) / 2.0
    sigma_value = midpoint / half_span
    rho_first = 1.0 / sigma_value
    rho_second = 1.0 / (2.0 * sigma_value - rho_first)
    return (midpoint, rho_second * rho_first, 2.0 * rho_second / half_span)


def row_ids(shape):
    return lax.broadcasted_iota(jnp.int32, shape, len(shape) - 2)


def lane_ids(shape):
    return lax.broadcasted_iota(jnp.int32, shape, len(shape) - 1)


def roll(value, shift, dim):
    size = value.shape[dim]
    shift = shift % size
    return value if shift == 0 else pltpu.roll(value, shift, dim)


def slot_place(slot, width):
    if width == 1:
        return slot, 0
    return 2 * (slot % 4), slot // 4


def slot_mask(slot, width):
    row, half = slot_place(slot, width)
    rows, lanes = row_ids((8, 128)), lane_ids((8, 128))
    mask = (rows >= row) & (rows < row + width)
    if width > 1:
        mask = mask & ((lanes >= 64) if half else (lanes < 64))
    return mask


def unpacked(tile, slot, width, low):
    row, half = slot_place(slot, width)
    rows, lanes = row_ids((8, 128)), lane_ids((8, 128))
    value = roll(tile, (8 - width if low else 0) - row, 0)
    if half:
        value = roll(value, 64, 1)
    mask = (rows >= 8 - width) if low else (rows < width)
    if width > 1:
        mask = mask & (lanes < 64)
    return jnp.where(mask, value, 0.0)


def pack_edges(block, width, high, low):
    planes, rows = block.shape[0] - 2 * width, block.shape[1] - 16
    for tile in range(planes // 8):
        upper = jnp.zeros((8, 128), jnp.float32)
        lower = upper
        for slot in range(8):
            row, half = slot_place(slot, width)
            mask = slot_mask(slot, width)
            plane = width + 8 * tile + slot
            last = roll(block[plane, rows : rows + 8, :], row + width - 8, 0)
            first = roll(block[plane, 8:16, :], row, 0)
            if half:
                last, first = roll(last, 64, 1), roll(first, 64, 1)
            upper = jnp.where(mask, last, upper)
            lower = jnp.where(mask, first, lower)
        high[tile] = upper
        low[tile] = lower


def unpack_edges(block, width, tile, low, high):
    rows = block.shape[1] - 16
    for slot in range(8):
        plane = width + 8 * tile + slot
        block[plane, 0:8, :] = unpacked(low, slot, width, True)
        block[plane, rows + 8 : rows + 16, :] = unpacked(high, slot, width, False)


def unpack_corners(block, width, side, low, high):
    planes, rows = block.shape[0] - 2 * width, block.shape[1] - 16
    for index in range(width):
        slot = 8 - width + index if side == 0 else index
        plane = index if side == 0 else planes + width + index
        block[plane, 0:8, :] = unpacked(low, slot, width, True)
        block[plane, rows + 8 : rows + 16, :] = unpacked(high, slot, width, False)


class Halo:
    def __init__(self, place, block, width, packs, sides, corners, send, recv):
        self.place, self.block, self.width = place, block, width
        self.packs, self.sides, self.corners = packs, sides, corners
        self.send, self.recv = send, recv
        self.planes = block.shape[0] - 2 * width
        self.rows = block.shape[1] - 16

    def clear(self):
        w, planes = self.width, self.planes
        edge = jnp.zeros((w,) + self.block.shape[1:], jnp.float32)
        self.block[0:w] = edge
        self.block[planes + w : planes + 2 * w] = edge
        self.sides[...] = jnp.zeros(self.sides.shape, jnp.float32)
        self.corners[...] = jnp.zeros(self.corners.shape, jnp.float32)

    def copy(self, number):
        dx, dy = NEAR[number]
        w, planes, rows, block = self.width, self.planes, self.rows, self.block
        if dy == 0:
            source = block.at[planes : planes + w] if dx > 0 else block.at[w : 2 * w]
            target = block.at[0:w] if dx > 0 else block.at[planes + w : planes + 2 * w]
            source, target = source.at[:, 8 : 8 + rows], target.at[:, 8 : 8 + rows]
        else:
            pack = self.packs.at[0 if dy > 0 else 1]
            if dx == 0:
                source, target = pack, self.sides.at[0 if dy > 0 else 1]
            else:
                source = pack.at[planes // 8 - 1 if dx > 0 else 0]
                target = self.corners.at[(0 if dx > 0 else 2) + (0 if dy > 0 else 1)]
        return pltpu.make_async_remote_copy(
            src_ref=source,
            dst_ref=target,
            send_sem=self.send.at[number],
            recv_sem=self.recv.at[number],
            device_id=self.place.device(dx, dy),
            device_id_type=MESH,
        )

    def start(self):
        for number, (dx, dy) in enumerate(NEAR):
            if dy == 0:
                pl.when(self.place.has(dx, dy))(lambda n=number: self.copy(n).start())
        pack_edges(self.block, self.width, self.packs.at[0], self.packs.at[1])
        for number, (dx, dy) in enumerate(NEAR):
            if dy != 0:
                pl.when(self.place.has(dx, dy))(lambda n=number: self.copy(n).start())

    def finish(self):
        self.arrive()
        for tile in range(self.planes // 8):
            unpack_edges(self.block, self.width, tile, self.sides[0, tile], self.sides[1, tile])
        for side in (0, 1):
            low, high = self.corners[2 * side], self.corners[2 * side + 1]
            unpack_corners(self.block, self.width, side, low, high)

    def arrive(self):
        for number, (dx, dy) in enumerate(NEAR):
            pl.when(self.place.has(-dx, -dy))(lambda n=number: self.copy(n).wait_recv())

    def drain(self):
        for number, (dx, dy) in enumerate(NEAR):
            pl.when(self.place.has(dx, dy))(lambda n=number: self.copy(n).wait_send())


class FineHalo(Halo):
    def __init__(self, place, block, packs, sides, corners, outer, send, recv):
        super().__init__(place, block, 1, packs, sides, corners, send, recv)
        self.outer = outer

    def clear(self):
        planes, rows = self.planes, self.rows
        edge = jnp.zeros((1,) + self.block.shape[1:], jnp.float32)
        self.block[0:1] = edge
        self.block[planes + 1 : planes + 2] = edge
        strip = jnp.zeros((planes + 2, 8, 128), jnp.float32)
        self.block[:, 0:8, :] = strip
        self.block[:, 8 + rows : 16 + rows, :] = strip
        for ref in (self.sides, self.corners, self.outer):
            ref[...] = jnp.zeros(ref.shape, jnp.float32)

    def copy(self, number):
        dx, dy = NEAR[number]
        if dy != 0:
            return super().copy(number)
        plane = self.planes if dx > 0 else 1
        return pltpu.make_async_remote_copy(
            src_ref=self.block.at[plane, 8 : 8 + self.rows],
            dst_ref=self.outer.at[0 if dx > 0 else 1, 8 : 8 + self.rows],
            send_sem=self.send.at[number],
            recv_sem=self.recv.at[number],
            device_id=self.place.device(dx, dy),
            device_id_type=MESH,
        )

    def finish(self, refined, scale):
        planes, rows = self.planes, self.rows
        for number, (dx, dy) in enumerate(NEAR):
            pl.when(self.place.has(-dx, -dy))(lambda n=number: self.copy(n).wait_recv())
        factor = refined * scale
        sides, ends = [], []
        for side in (0, 1):
            strip = self.sides[side].reshape(planes, 128)
            at = row_ids(strip.shape)
            before = jnp.where(at == 0, 0.0, roll(strip, 1, 0))
            after = jnp.where(at == planes - 1, 0.0, roll(strip, -1, 0))
            sides.append(factor * along_lanes((before + after) + (strip + strip), True))
        for end in (0, 1):
            slot = 7 if end == 0 else 0
            low, high = self.corners[2 * end], self.corners[2 * end + 1]
            plane = jnp.concatenate(
                [
                    unpacked(low, slot, 1, True),
                    self.outer[end, 8 : 8 + rows, :],
                    unpacked(high, slot, 1, False),
                ],
                axis=0,
            )
            total = (roll(plane, 1, 0) + roll(plane, -1, 0)) + (plane + plane)
            ends.append(factor * along_lanes(total[8 : 8 + rows], True))
        return sides, ends


def edge_tile(strip, plane, last):
    base = plane // 8 * 8
    value = roll(strip[base : base + 8], (7 if last else 0) - plane % 8, 0)
    return jnp.where(row_ids((8, 128)) == (7 if last else 0), value, 0.0)


class Coefficients(Halo):
    def __init__(self, place, fields, packs, ends, sides, corners, outer, send, recv):
        self.place, self.fields = place, fields
        self.packs, self.ends = packs, ends
        self.sides, self.corners, self.outer = sides, corners, outer
        self.send, self.recv = send, recv

    def clear(self):
        for ref in (self.sides, self.corners, self.outer):
            ref[...] = jnp.zeros(ref.shape, jnp.float32)

    def copy(self, number):
        dx, dy = NEAR[number]
        across, along = (0 if dx > 0 else 1), (0 if dy > 0 else 1)
        if dy == 0:
            source, target = self.ends.at[across], self.outer.at[across]
        else:
            source = self.packs.at[along]
            target = self.sides.at[along] if dx == 0 else self.corners.at[2 * across + along]
        return pltpu.make_async_remote_copy(
            src_ref=source,
            dst_ref=target,
            send_sem=self.send.at[number],
            recv_sem=self.recv.at[number],
            device_id=self.place.device(dx, dy),
            device_id_type=MESH,
        )

    def start(self, tiles):
        self.tiles = tiles
        at = 0
        for block in self.fields:
            size = (block.shape[0] - 4) // 8
            part = pl.ds(at, size)
            pack_edges(block, 2, self.packs.at[0, part], self.packs.at[1, part])
            at += size
        at = 0
        for block in self.fields:
            planes, rows = block.shape[0] - 4, block.shape[1] - 16
            size = rows // 8
            for index in range(2):
                for across, plane in ((0, planes + index), (1, 2 + index)):
                    value = block[plane, 8 : 8 + rows, :].reshape(size, 8, 128)
                    self.ends[across, at : at + size] = value
                at += size
        for ref in (self.packs, self.ends):
            for index in range(2):
                for where, tile in enumerate(tiles):
                    ref[index, ref.shape[1] - 2 + where] = tile
        for number, (dx, dy) in enumerate(NEAR):
            pl.when(self.place.has(dx, dy))(lambda n=number: self.copy(n).start())

    def finish(self, second):
        self.arrive()
        at, end = 0, 0
        for block in self.fields:
            planes, rows = block.shape[0] - 4, block.shape[1] - 16
            count, size = planes // 8, rows // 8
            for tile in range(count):
                low, high = self.sides[0, at + tile], self.sides[1, at + tile]
                unpack_edges(block, 2, tile, low, high)
            for side in (0, 1):
                tile = at + (count - 1 if side == 0 else 0)
                low, high = self.corners[2 * side, tile], self.corners[2 * side + 1, tile]
                unpack_corners(block, 2, side, low, high)
                for index in range(2):
                    plane = index if side == 0 else planes + 2 + index
                    first = end + index * size
                    value = self.outer[side, first : first + size].reshape(rows, 128)
                    block[plane, 8 : 8 + rows, :] = value
            at += count
            end += 2 * size
        around = []
        for part in range(2):
            side, last = at + part, end + part
            around.append(
                [
                    [self.corners[0, side], self.outer[0, last], self.corners[1, side]],
                    [self.sides[0, side], self.tiles[part], self.sides[1, side]],
                    [self.corners[2, side], self.outer[1, last], self.corners[3, side]],
                ]
            )
        lay_out(around, second)


def fold(values):
    tiles = []
    for part in range(2):
        planes = [roll(values[32 * part + 8 * at : 32 * part + 8 * at + 8], 32 * at, 1) for at in range(4)]
        tiles.append((planes[0] + planes[1]) + (planes[2] + planes[3]))
    return tiles


def lay_out(around, field):
    lanes = lane_ids((8, 128))
    for bx in range(3):
        for by in range(3):
            for index in range(8):
                value = roll(around[index // 4][bx][by], -32 * (index % 4), 1)
                value = jnp.where(lanes < 32, value, 0.0)
                field[8 * bx + index, 8 * by : 8 * by + 8, :] = value


class Gather(Halo):
    def __init__(self, place, tiles, send, recv):
        self.place, self.tiles, self.send, self.recv = place, tiles, send, recv

    def clear(self):
        self.tiles[...] = jnp.zeros(self.tiles.shape, jnp.float32)

    def copy(self, number):
        dx, dy = NEAR[number]
        return pltpu.make_async_remote_copy(
            src_ref=self.tiles.at[1, 1],
            dst_ref=self.tiles.at[1 - dx, 1 - dy],
            send_sem=self.send.at[number],
            recv_sem=self.recv.at[number],
            device_id=self.place.device(dx, dy),
            device_id_type=MESH,
        )

    def start(self):
        for number, (dx, dy) in enumerate(NEAR):
            pl.when(self.place.has(dx, dy))(lambda n=number: self.copy(n).start())


class Place:
    def __init__(self, counts):
        self.counts = counts
        self.box, self.agg = lax.axis_index("box"), lax.axis_index("agg")

    def device(self, dx, dy):
        return (self.box + dx, self.agg + dy)

    def has(self, dx, dy):
        x, y = self.device(dx, dy)
        return (x >= 0) & (x < self.counts[0]) & (y >= 0) & (y < self.counts[1])

    def greet(self):
        semaphore = pltpu.get_barrier_semaphore()
        for dx, dy in NEAR:

            @pl.when(self.has(dx, dy))
            def _(dx=dx, dy=dy):
                pl.semaphore_signal(
                    semaphore, inc=1, device_id=self.device(dx, dy), device_id_type=MESH
                )

    def await_greetings(self):
        spans = []
        for at, count in zip((self.box, self.agg), self.counts):
            spans.append(1 + jnp.minimum(at, 1) + jnp.minimum(count - 1 - at, 1))
        pl.semaphore_wait(pltpu.get_barrier_semaphore(), spans[0] * spans[1] - 1)


def along_lanes(total, wrap):
    left, right = roll(total, 1, 1), roll(total, -1, 1)
    if wrap:
        lanes = lane_ids(total.shape)
        left = jnp.where(lanes == 0, 0.0, left)
        right = jnp.where(lanes == 127, 0.0, right)
    return (left + right) + (total + total)


def weighted(block, start, count, wrap):
    held = [block[start - 1 + index] for index in range(count + 2)]
    pairs = [low + high for low, high in zip(held[:-1], held[1:])]
    results = []
    for index in range(count):
        total = pairs[index] + pairs[index + 1]
        total = (roll(total, 1, 0) + roll(total, -1, 0)) + (total + total)
        middle = held[index + 1]
        if wrap:
            total, middle = total[8:-8], middle[8:-8]
        results.append((along_lanes(total, wrap), middle))
    return results


def pair_matrix(extent):
    source, target = row_ids((256, 128)) % 128, lane_ids((256, 128))
    pairs = (source < extent) & ((source == 2 * target) | (source == 2 * target + 1))
    return jnp.where(pairs, 0.5, 0.0).astype(jnp.bfloat16)


def paired(flat, matrix):
    half = flat.shape[0] // 2
    rows = flat[pl.ds(0, half, stride=2), :] + flat[pl.ds(1, half, stride=2), :]
    high = rows.astype(jnp.bfloat16)
    low = (rows - high.astype(jnp.float32)).astype(jnp.bfloat16)
    return jnp.dot(
        jnp.concatenate([high, low], axis=1),
        matrix[...],
        preferred_element_type=jnp.float32,
    )


def in_grid(start, stop, shape, extent):
    rows, lanes = row_ids(shape), lane_ids(shape)
    return jnp.where((rows >= start) & (rows < stop) & (lanes < extent), 1.0, 0.0)


def plane_in_grid(index, count):
    return jnp.where((index >= 0) & (index < count), 1.0, 0.0)


def groups(start, count, size, body):
    assert count % size == 0
    if count == size:
        body(start)
        return

    def step(index, _):
        body(start + index * size)
        return 0

    lax.fori_loop(0, count // size, step, 0)


def kernel(
    counts,
    flags_in, source_in, guess_in, reaction_in,
    iterate, out_one, out_two, out_three, out_four, out_bottom,
    flags, source, reaction,
    field_a, field_b, field_c, outer, matrices,
    f_one, k_one, e_one, f_two, k_two, e_two,
    f_three, k_three, e_three, f_four, k_four, e_four,
    flat_zero, flat_one, flat_two, flat_three, flat_extra,
    packs_zero, sides_zero, packs_one, sides_one, corners,
    k_packs, k_ends, k_sides, k_corners, k_outer, tiles_two, tiles_four, held_one, held_two, held_three, held_four, held_bottom,
    near_send, near_recv, local,
):
    place = Place(counts)
    planes, rows, depth = source.shape

    def halo(number, block, width, packs, sides, index):
        return Halo(
            place, block, width, packs.at[index], sides.at[index], corners.at[number],
            near_send.at[number], near_recv.at[number],
        )

    halo_a, halo_b, halo_c = (
        FineHalo(
            place, block, packs_zero.at[index], sides_zero.at[index], corners.at[index],
            outer.at[index], near_send.at[index], near_recv.at[index],
        )
        for index, block in enumerate((field_a, field_b, field_c))
    )
    halo_f_one = halo(3, f_one, 2, packs_one, sides_one, 0)
    gather_two = Gather(place, tiles_two, near_send.at[4], near_recv.at[4])
    halo_k = Coefficients(
        place, (k_one,), k_packs, k_ends, k_sides, k_corners, k_outer,
        near_send.at[5], near_recv.at[5],
    )
    gather_four = Gather(place, tiles_four, near_send.at[6], near_recv.at[6])
    own_a = field_a.at[1 : 1 + planes, 8 : 8 + rows]
    own_c = field_c.at[1 : 1 + planes, 8 : 8 + rows]
    quarter = planes // 4
    parts = [pl.ds(index * quarter, quarter) for index in range(4)]
    pairs = [(guess_in.at[part], own_a.at[part]) for part in parts]
    pairs += [(flags_in, flags)]
    pairs += [(reaction_in.at[part], reaction.at[part]) for part in parts]
    pairs += [(source_in.at[part], source.at[part]) for part in parts]
    loads = [
        pltpu.make_async_copy(origin, target, local.at[6 + index])
        for index, (origin, target) in enumerate(pairs)
    ]
    stores = [
        pltpu.make_async_copy(origin, target, local.at[index])
        for index, (origin, target) in enumerate(
            (
                (own_c, iterate), (held_one, out_one), (held_two, out_two),
                (held_three, out_three), (held_four, out_four), (held_bottom, out_bottom),
            )
        )
    ]
    for load in loads[:4]:
        load.start()
    for exchange in (
        halo_a, halo_b, halo_c, halo_f_one, gather_two, halo_k, gather_four,
    ):
        exchange.clear()
    place.greet()
    flat_two[...] = jnp.zeros(flat_two.shape, jnp.float32)
    flat_extra[...] = jnp.zeros(flat_extra.shape, jnp.float32)
    for load in loads[4:]:
        load.start()
    for level in range(LEVELS):
        matrices[level] = pair_matrix(depth >> level)
    for load in loads[:4]:
        load.wait()
    place.await_greetings()
    halo_a.start()

    def spread(flat, target, count, level):
        values = paired(flat, matrices.at[level])
        target[2 : 2 + count, 8 : 8 + count, :] = values.reshape(count, count, 128)

    def put(flat, plane, size, value):
        flat[pl.ds(pl.multiple_of(plane * size, size), size), :] = value

    one, two, three = planes // 2, planes // 4, planes // 8
    for load in loads[4:9]:
        load.wait()

    def coarse_reaction(start):
        for plane in range(4):
            at = start + plane
            put(flat_zero, at, rows, reaction[2 * at] + reaction[2 * at + 1])

    groups(0, one, 4, coarse_reaction)
    spread(flat_zero, k_one, one, 0)
    for load in loads[9:]:
        load.wait()

    lanes = lane_ids((1, depth))
    patch = depth // flags.shape[2]
    refined = jnp.zeros((1, depth), jnp.float32)
    for box in range(flags.shape[2]):
        chosen = (lanes >= box * patch) & (lanes < (box + 1) * patch)
        flag = flags[0, :, box : box + 1].astype(jnp.float32)
        refined = refined + jnp.where(chosen, flag, 0.0)

    midpoint, factor_one, factor_two = coefficients(0)

    def fine_residuals(block, start, count):
        results = []
        for index, (total, middle) in enumerate(weighted(block, start + 1, count, True)):
            applied = (8.0 / 7.0 + reaction[start + index]) * middle - total * (1.0 / 56.0)
            results.append((refined * (source[start + index] - applied), middle))
        return results

    def add_edges(block, shares):
        (low, high), ends = shares
        for plane in range(planes):
            block[plane + 1, 8:16, :] += edge_tile(low, plane, False)
            block[plane + 1, rows : 8 + rows, :] += edge_tile(high, plane, True)
        block[1, 8 : 8 + rows, :] += ends[0]
        block[planes, 8 : 8 + rows, :] += ends[1]

    def first(start):
        for index, (residual, middle) in enumerate(fine_residuals(field_a, start, 16)):
            field_b[start + index + 1, 8 : 8 + rows, :] = middle + residual * (1.0 / midpoint)

    groups(0, planes, 16, first)
    add_edges(field_b, halo_a.finish(refined, 1.0 / (56.0 * midpoint)))
    halo_b.start()

    for plane in range(two):
        put(
            flat_one, plane, one,
            k_one[2 + 2 * plane, 8 : 8 + one, :] + k_one[3 + 2 * plane, 8 : 8 + one, :],
        )
    k_tiles = fold(paired(flat_one, matrices.at[1]))
    halo_k.start(k_tiles)

    def second(start):
        for index, (residual, middle) in enumerate(fine_residuals(field_b, start, 16)):
            before = field_a[start + index + 1, 8 : 8 + rows, :]
            step = factor_one * (middle - before) + factor_two * residual
            field_c[start + index + 1, 8 : 8 + rows, :] = middle + step

    groups(0, planes, 16, second)
    halo_a.drain()
    add_edges(field_c, halo_b.finish(refined, factor_two / 56.0))
    halo_c.start()
    stores[0].start()

    def third(start):
        values = fine_residuals(field_c, 2 * start, 16)
        for index in range(8):
            put(flat_zero, start + index, rows, values[2 * index][0] + values[2 * index + 1][0])

    groups(0, one, 8, third)
    halo_b.drain()
    (low, high), ends = halo_c.finish(refined, 1.0 / 56.0)
    for plane in range(one):
        at = plane * rows
        for strip, last, begin in ((low, False, at), (high, True, at + rows - 8)):
            both = edge_tile(strip, 2 * plane, last) + edge_tile(strip, 2 * plane + 1, last)
            flat_zero[begin : begin + 8, :] += both
    flat_zero[0:rows, :] += ends[0]
    flat_zero[(one - 1) * rows : one * rows, :] += ends[1]
    spread(flat_zero, f_one, one, 0)
    halo_f_one.start()

    halo_k.finish(k_two)
    for plane in range(12):
        flat_extra[32 * plane : 32 * plane + 24, :] = k_two[2 * plane] + k_two[2 * plane + 1]
    k_three[...] = paired(flat_extra, matrices.at[2]).reshape(12, 16, 128)
    for plane in range(6):
        flat_three[16 * plane : 16 * plane + 16, :] = k_three[2 * plane] + k_three[2 * plane + 1]
    k_four[...] = paired(flat_three, matrices.at[3]).reshape(6, 8, 128)
    halo_c.drain()
    halo_k.drain()

    def correct(level, f, k, e, start, count, mask):
        midpoint, factor_one, factor_two = coefficients(level)
        slope = factor_two / midpoint
        keep = (1.0 + factor_one) / midpoint + factor_two - slope * 8.0 / 7.0
        for index, (total, middle) in enumerate(weighted(f, start, count, False)):
            plane = start + index
            value = (keep - slope * k[plane]) * middle + (slope / 56.0) * total
            e[plane] = value * mask(plane)

    def left_over(f, k, e, start, count):
        return [
            f[start + index]
            - ((8.0 / 7.0 + k[start + index]) * middle - total * (1.0 / 56.0))
            for index, (total, middle) in enumerate(weighted(e, start, count, False))
        ]

    halo_f_one.finish()
    mask_one = in_grid(
        8 - place.agg * one, 8 + (counts[1] - place.agg) * one, f_one.shape[1:], depth // 2
    )

    def at_one(plane):
        return mask_one * plane_in_grid(place.box * one + plane - 2, counts[0] * one)

    groups(1, one + 2, 18, lambda start: correct(1, f_one, k_one, e_one, start, 18, at_one))

    def remainder(start):
        values = left_over(f_one, k_one, e_one, 2 * start + 2, 16)
        for index in range(8):
            total = values[2 * index] + values[2 * index + 1]
            put(flat_one, start + index, one, total[8 : 8 + one])

    groups(0, two, 8, remainder)
    for part, tile in enumerate(fold(paired(flat_one, matrices.at[1]))):
        tiles_two[1, 1, part] = tile
    gather_two.start()
    held_one[...] = e_one[2 : 2 + one, 8 : 8 + one, 0 : depth // 2]
    stores[1].start()
    halo_f_one.drain()

    mask_two = in_grid(
        8 - place.agg * two, 8 + (counts[1] - place.agg) * two, f_two.shape[1:], depth // 4
    )

    def at_two(plane):
        return mask_two * plane_in_grid(place.box * two + plane - 8, counts[0] * two)

    gather_two.arrive()
    lay_out(
        [
            [[tiles_two[bx, by, part] for by in range(3)] for bx in range(3)]
            for part in range(2)
        ],
        f_two,
    )
    correct(2, f_two, k_two, e_two, 3, 18, at_two)
    values = left_over(f_two, k_two, e_two, 4, 16)
    for plane in range(8):
        total = values[2 * plane] * at_two(4 + 2 * plane)
        total = total + values[2 * plane + 1] * at_two(5 + 2 * plane)
        flat_two[32 * plane : 32 * plane + 24, :] = total
    f_three[2:10] = paired(flat_two, matrices.at[2]).reshape(8, 16, 128)

    mask_three = in_grid(
        4 - place.agg * three, 4 + (counts[1] - place.agg) * three, f_three.shape[1:], depth // 8
    )

    def at_three(plane):
        return mask_three * plane_in_grid(place.box * three + plane - 4, counts[0] * three)

    correct(3, f_three, k_three, e_three, 3, 6, at_three)
    values = left_over(f_three, k_three, e_three, 4, 4)
    for plane in range(2):
        flat_three[16 * plane : 16 * plane + 16, :] = values[2 * plane] + values[2 * plane + 1]
    tiles_four[1, 1] = paired(flat_three.at[0:32], matrices.at[3]).reshape(2, 8, 128)
    gather_four.start()
    held_three[...] = e_three[4:8, 4:8, 0 : depth // 8]
    stores[3].start()
    held_two[...] = e_two[8 : 8 + two, 8 : 8 + two, 0 : depth // 4]
    stores[2].start()
    gather_two.drain()

    four = three // 2
    mask_four = in_grid(
        2 - place.agg * four, 2 + (counts[1] - place.agg) * four, f_four.shape[1:], depth // 16
    )

    def at_four(plane):
        return mask_four * plane_in_grid(place.box * four + plane - 2, counts[0] * four)

    gather_four.arrive()
    ids = row_ids((8, 128))
    for plane in range(6):
        before, own, after = (tiles_four[plane // 2, by, plane % 2] for by in range(3))
        value = jnp.where(ids < 4, own, roll(after, 2, 0))
        value = jnp.where(ids < 2, roll(before, -2, 0), value)
        f_four[plane] = jnp.where(ids < 6, value, 0.0)
    correct(4, f_four, k_four, e_four, 1, 4, at_four)
    held_four[...] = e_four[2:4, 2:4, 0 : depth // 16]
    stores[4].start()
    for index, value in enumerate(left_over(f_four, k_four, e_four, 2, 2)):
        held_bottom[index] = value[2:4, 0 : depth // 16]
    stores[5].start()
    gather_four.drain()
    for store in stores:
        store.wait()


def hand_on(*refs):
    sources, targets, held = refs[0:6], refs[6:12], refs[12:18]
    semaphores = refs[18]
    size = sources[0].shape[0] // 4
    parts = [(0, pl.ds(piece * size, size)) for piece in range(4)]
    parts += [(index, pl.ds(0, sources[index].shape[0])) for index in range(1, 6)]
    inward, outward = [], []
    for number, (index, part) in enumerate(parts):
        inner = held[index].at[part]
        inward.append(
            pltpu.make_async_copy(sources[index].at[part], inner, semaphores.at[0, number])
        )
        outward.append(
            pltpu.make_async_copy(inner, targets[index].at[part], semaphores.at[1, number])
        )
    for copy in inward:
        copy.start()
    for before, after in zip(inward, outward):
        before.wait()
        after.start()
    for copy in outward:
        copy.wait()


def per_device(counts, source, guess, reaction, flags):
    planes, rows, depth = source.shape
    assert planes == rows and planes == 32 and depth == 128 and flags.shape[:2] == (1, 1)
    f32 = jnp.float32

    def vmem(*shape):
        return pltpu.VMEM(shape, f32)

    one, two = planes // 2, planes // 4
    scratch = [pltpu.VMEM(flags.shape, jnp.int32)] + [vmem(planes, rows, depth)] * 2
    scratch += [vmem(planes + 2, rows + 16, depth)] * 3 + [vmem(3, 2, rows + 16, depth)]
    scratch += [pltpu.VMEM((LEVELS, 256, 128), jnp.bfloat16)]
    scratch += [vmem(one + 4, one + 16, 128)] * 3 + [vmem(24, 24, 128)] * 3
    scratch += [vmem(12, 16, 128)] * 3 + [vmem(6, 8, 128)] * 3
    scratch += [vmem(one * rows, 128), vmem(two * one, 128), vmem(256, 128)]
    scratch += [vmem(96, 128), vmem(384, 128)]
    scratch += [vmem(3, 2, planes // 8, 8, 128)] * 2
    scratch += [vmem(1, 2, one // 8, 8, 128)] * 2
    k_tiles = one // 8 + 2
    k_planes = 2 * (one // 8) + 2
    scratch += [vmem(4, 4, 8, 128), vmem(2, k_tiles, 8, 128), vmem(2, k_planes, 8, 128)]
    scratch += [vmem(2, k_tiles, 8, 128), vmem(4, k_tiles, 8, 128), vmem(2, k_planes, 8, 128)]
    scratch += [vmem(3, 3, 2, 8, 128)] * 2
    outs = [jax.ShapeDtypeStruct(source.shape, f32)]
    for level in range(1, LEVELS + 1):
        outs.append(
            jax.ShapeDtypeStruct((planes >> level, rows >> level, depth >> level), f32)
        )
    outs.append(outs[-1])
    scratch += [vmem(*out.shape) for out in outs[1:]]
    scratch += [pltpu.SemaphoreType.DMA((7, 8))] * 2
    scratch += [pltpu.SemaphoreType.DMA((19,))]
    anywhere = pl.BlockSpec(memory_space=pl.ANY)
    results = pl.pallas_call(
        functools.partial(kernel, counts),
        out_shape=outs,
        in_specs=[anywhere] * 4,
        out_specs=[anywhere] * 6,
        scratch_shapes=scratch,
        compiler_params=pltpu.CompilerParams(
            collective_id=0, has_side_effects=True, vmem_limit_bytes=60 * 1024 * 1024
        ),
    )(flags, source, guess, reaction)
    return tuple(
        pl.pallas_call(
            hand_on,
            out_shape=outs,
            in_specs=[anywhere] * 6,
            out_specs=[anywhere] * 6,
            scratch_shapes=[vmem(*out.shape) for out in outs] + [pltpu.SemaphoreType.DMA((2, 9))],
            compiler_params=pltpu.CompilerParams(vmem_limit_bytes=60 * 1024 * 1024),
        )(*results)
    )


def solution(mesh):
    spec = P("box", "agg", None)
    counts = (mesh.shape["box"], mesh.shape["agg"])
    return jax.shard_map(
        functools.partial(per_device, counts),
        mesh=mesh,
        in_specs=(spec,) * 4,
        out_specs=(spec,) * 6,
        check_vma=False,
    )
```
